256 devices in a mesh: row: 8 (over z_lo, x), col: 32 (over y, z_hi, core).
Axes of the slice: x: 4, y: 4, z: 8 (z_hi: 4, z_lo: 2; z = z_hi * 2 + z_lo), core: 2. Of those that a mesh axis runs over, the one named last changes fastest.
Arguments:
- adj_trailing: float32 [8192, 8192], P('row', 'col'), may hold values from -6 to 6
- panel: float32 [8192, 512], P('row', 'col'), may hold values from -0.0625 to 0.0625
- panel_adjoint: float32 [8192, 512], P('row', 'col'), may hold values from -6 to 6
- inverse_diag: float32 [512, 512], replicated, as said below
Outputs:
- grad_block: float32 [8192, 512], P('row', 'col')
- diag_grad: float32 [512, 512], P('col')
The draws below stay inside these ranges and needn't reach their ends.
Inputs may be any that keep to these rules, and one draw needn't show every extreme that they name: `inverse_diag`: lower triangular, with a diagonal of 0.5 to 1.5.
All inputs are finite; a program needn't handle non-finite values.
Results may differ from the reference program's by a relative error of at most 0.000088.
Values sent between devices are 32-bit elements; how exact they have to be, the bound alone decides.
A program may use at most 64 MiB of HBM per device.

```python
import jax
import jax.numpy as jnp
from jax import lax

M = 8192
B = 512
NB = 64
N_ROW = 8
N_COL = 32


def draw_inverse_diag(key, part):
    key = jax.random.fold_in(key, 7)
    key_diag, key_off = jax.random.split(key, 2)
    diag = jax.random.uniform(key_diag, (B,), jnp.float32, 0.5, 1.5)
    off = 0.7 * jax.random.normal(key_off, (B, B), jnp.float32) / jnp.sqrt(jnp.float32(B))
    return jnp.tril(off, -1) + jnp.diag(diag)


def steps_of(key, dims, shards, smallest, high):
    gain = 1.0
    for axis_at, blocks in shards:
        draws = jax.random.uniform(jax.random.fold_in(jax.random.fold_in(key, 6), axis_at), (blocks,), jnp.float32, smallest / len(shards), high / len(shards))
        gain = gain * jnp.repeat(jnp.exp(draws), dims[axis_at] // blocks).reshape((-1,) + (1,) * (len(dims) - 1 - axis_at))
    return gain


def gaussian(key, shape, deviation, most, pieces=(), kind=jnp.bfloat16):
    factor_of = steps_of(key, shape, pieces, -0.22, 0.18) if pieces else 1.0
    array = jax.random.normal(key, shape, jnp.float32) * deviation * factor_of
    return jnp.minimum(jnp.maximum(array, -most), most).astype(kind)


def setup_inputs(seed: int = 0) -> dict:
    key_list = jax.random.split(jax.random.key(seed), 5)
    adj_trailing = gaussian(key_list[0], (M, M), 1.0, 6.0, ((0, 8), (1, 32)), jnp.float32)
    panel = gaussian(key_list[1], (M, B), M ** -0.5, 0.0625, ((0, 8), (1, 32)), jnp.float32)
    panel_adjoint = gaussian(key_list[2], (M, B), 1.0, 6.0, ((0, 8), (1, 32)), jnp.float32)
    inverse_diag = draw_inverse_diag(jax.random.fold_in(key_list[4], 71), 0)
    return {"adj_trailing": adj_trailing, "panel": panel, "panel_adjoint": panel_adjoint, "inverse_diag": inverse_diag}


def stored_to_natural(count, parts):
    per = count // parts
    spots = jnp.arange(count, dtype=jnp.int32)
    owner = spots // per
    within = spots % per
    return ((within // NB) * parts + owner) * NB + within % NB


def natural_to_stored(natural, count, parts):
    per = count // parts
    block = natural // NB
    return ((block % parts) * per + (block // parts) * NB + natural % NB).astype(jnp.int32)


def reference(adj_trailing, panel, panel_adjoint, inverse_diag):
    highest = lax.Precision.HIGHEST
    row_nat = stored_to_natural(M, N_ROW)
    col_nat = stored_to_natural(M, N_COL)
    lowered = jnp.where(row_nat[:, None] >= col_nat[None, :], adj_trailing, jnp.zeros((), adj_trailing.dtype))
    col_panel = panel[natural_to_stored(col_nat, M, N_ROW)]
    lower_term = jnp.dot(lowered, col_panel, precision=highest)
    mirror_term = jnp.dot(lowered.T, panel, precision=highest)
    mirror_rows = mirror_term[natural_to_stored(row_nat, M, N_COL)]
    adjoint = panel_adjoint - (lower_term + mirror_rows)
    grad_block = jnp.dot(adjoint, inverse_diag, precision=highest)
    diag_grad = -jnp.tril(jnp.dot(grad_block.T, panel, precision=highest))
    return grad_block, diag_grad
```

```python
import functools

import jax
import jax.numpy as jnp
from jax import lax
from jax.experimental import pallas as pl
from jax.experimental.pallas import tpu as pltpu
from jax.sharding import PartitionSpec as P

F32 = jnp.float32
BF16 = jnp.bfloat16
MESH = pl.DeviceIdType.MESH
NT = (((1,), (1,)), ((), ()))


def split(value):
    high = value.astype(BF16)
    low = (value - high.astype(F32)).astype(BF16)
    return high, low


def dot3(a_high, a_low, b_high, b_low):
    def one(a, b):
        return lax.dot_general(a, b, NT, preferred_element_type=F32)

    return one(a_high, b_low) + one(a_low, b_high) + one(a_high, b_high)


def aligned(start, size):
    return pl.ds(pl.multiple_of(start, size), size)


def kernel(
    a_hbm, panel_hbm, pa_hbm, inv_hbm, grad_ref, diag_ref,
    panel_v, pa_v, inv_v, wide, s_raw, pf, pc, s_hi, s_lo, st_hi, st_lo,
    p_hi, p_lo, f_hi, f_lo, inv_r, it_hi, it_lo, pa_r, out1, out2, ry, t1, rz, rr,
    q_sum, rq, adj, gt, rg, gfull, dpart, rd,
    local_sem, agz_s, agz_r, agy_s, agy_r, sa_s, sa_r, pc_s, pc_r, po_s, po_r,
    ry_s, ry_r, rr_s, rr_r, q_s, q_r, rz_s, rz_r, f_s, f_r, rg_s, rg_r, rd_s, rd_r,
):
    r = lax.axis_index("row")
    c = lax.axis_index("col")
    zl, x = r // 4, r % 4
    y, z, p = c // 8, (c // 2) % 4, c % 2
    yz = y * 4 + z

    def dev(zl_, x_, y_, z_, p_):
        return (zl_ * 4 + x_, (y_ * 4 + z_) * 2 + p_)

    def remote(src, dst, send, recv, target):
        return pltpu.make_async_remote_copy(
            src_ref=src, dst_ref=dst, send_sem=send, recv_sem=recv,
            device_id=target, device_id_type=MESH,
        )

    sibling = dev(zl, x, y, z, 1 - p)

    barrier = pltpu.get_barrier_semaphore()
    greet = [sibling]
    greet += [dev(zl, x, y, (z + j) % 4, p) for j in (1, 2, 3)]
    greet += [dev(zl, x, (y + j) % 4, z, p) for j in (1, 2, 3)]
    row_offsets = [(a, b) for a in (0, 1) for b in (0, 1, 2, 3) if (a, b) != (0, 0)]
    greet += [dev((zl + a) % 2, (x + b) % 4, y, z, p) for a, b in row_offsets]
    for target in greet:
        pl.semaphore_signal(barrier, inc=1, device_id=target, device_id_type=MESH)

    load_panel = pltpu.make_async_copy(panel_hbm, panel_v, local_sem.at[0])
    load_a = pltpu.make_async_copy(a_hbm, s_raw.at[p], local_sem.at[1])
    load_pa = pltpu.make_async_copy(pa_hbm, pa_v, local_sem.at[2])
    load_inv = pltpu.make_async_copy(inv_hbm, inv_v, local_sem.at[3])
    load_panel.start()
    load_a.start()
    load_pa.start()
    load_inv.start()

    wide[...] = jnp.zeros_like(wide)
    adj[...] = jnp.zeros_like(adj)
    load_panel.wait()
    wide[:, 0:16] = panel_v[...]
    for t in range(8):
        w1 = (2 * t) // 4 + 4 * ((2 * t) % 4)
        w2 = (2 * t + 1) // 4 + 4 * ((2 * t + 1) % 4)
        both = jnp.concatenate([wide[w1 * 64:w1 * 64 + 64, :], wide[w2 * 64:w2 * 64 + 64, :]], axis=0)
        pf[yz, p, :, 128 * t:128 * t + 128] = both.T[0:16, :]

    pl.semaphore_wait(barrier, len(greet))

    sends = []

    for j in (1, 3, 2):
        cp = remote(pf.at[yz, p], pf.at[yz, p], agz_s.at[j], agz_r.at[j], dev(zl, x, y, (z + j) % 4, p))
        cp.start()
        sends.append(cp)

    def forward_y(k):
        slot = y * 4 + (z + 4 - k) % 4
        for j in (1, 3, 2):
            cp = remote(
                pf.at[slot, p], pf.at[slot, p], agy_s.at[j, k], agy_r.at[j, k],
                dev(zl, x, (y + j) % 4, z, p),
            )
            cp.start()
            sends.append(cp)

    forward_y(0)
    load_a.wait()
    cp_a = remote(s_raw.at[p], s_raw.at[p], sa_s, sa_r, sibling)
    cp_a.start()

    lane = lax.broadcasted_iota(jnp.int32, (128, 256), 1)
    line = lax.broadcasted_iota(jnp.int32, (128, 256), 0)

    def prepare_s(b):
        c_b = c - p + b
        col_nat = (32 * (lane // 64) + c_b) * 64 + lane % 64

        def step(t, carry):
            y2 = t // 2
            z2 = (t % 2) * 2
            w1 = y2 + 4 * z2
            w2 = w1 + 4
            rows = jnp.concatenate(
                [s_raw[b, aligned(64 * w1, 64), :], s_raw[b, aligned(64 * w2, 64), :]], axis=0
            )
            first = (8 * w1 + r) * 64
            row_nat = first + line + jnp.where(line >= 64, 32 * 64 - 64, 0)
            value = jnp.where(row_nat >= col_nat, rows, 0.0)
            high, low = split(value)
            s_hi[aligned(128 * t, 128), aligned(256 * b, 256)] = high
            s_lo[aligned(128 * t, 128), aligned(256 * b, 256)] = low
            high, low = split(value.T)
            st_hi[aligned(256 * b, 256), aligned(128 * t, 128)] = high
            st_lo[aligned(256 * b, 256), aligned(128 * t, 128)] = low
            return carry

        lax.fori_loop(0, 8, step, 0)

    prepare_s(p)

    for k in (1, 3, 2):
        slot = y * 4 + (z + 4 - k) % 4
        remote(pf.at[slot, p], pf.at[slot, p], agz_s.at[k], agz_r.at[k], sibling).wait_recv()
        forward_y(k)

    x0 = 2 * (z % 2)
    zr = z // 2
    dx = (x + 4 - x0) % 4
    top = zl == zr
    conditional = []

    def spread(j):
        group = (y + 4 - j) % 4
        block = aligned(group * 64, 64)

        for b in (0, 1):
            part = pc.at[block, pl.ds(256 * b, 256)]
            root = jnp.logical_and(top, dx == b)

            @pl.when(root)
            def _():
                for i in range(4):
                    pc[aligned(group * 64 + 16 * i, 16), 256 * b:256 * b + 256] = pf[
                        group * 4 + i, p, :, aligned(256 * y, 256)
                    ]

            @pl.when(jnp.logical_not(root))
            def _():
                remote(part, part, pc_s.at[b, j, 0], pc_r.at[b, j], sibling).wait_recv()

            over = remote(part, part, pc_s.at[b, j, 0], pc_r.at[b, j], dev(1 - zl, x, y, z, p))
            up = remote(part, part, pc_s.at[b, j, 1], pc_r.at[b, j], dev(zl, (x + 1) % 4, y, z, p))
            down = remote(part, part, pc_s.at[b, j, 2], pc_r.at[b, j], dev(zl, (x + 3) % 4, y, z, p))
            if b == 0:
                go_up = dx == 0
                go_down = jnp.logical_or(dx == 0, dx == 3)
            else:
                go_up = jnp.logical_or(dx == 1, dx == 2)
                go_down = dx == 1
            for cond, cp in ((root, over), (go_up, up), (go_down, down)):
                pl.when(cond)(cp.start)
                conditional.append((cond, cp))

    def to_sibling(j):
        group = (y + 4 - j) % 4
        part = pf.at[pl.ds(group * 4, 4), p]
        cp = remote(part, part, po_s.at[j], po_r.at[j], sibling)
        cp.start()
        sends.append(cp)

    spread(0)
    to_sibling(0)

    remote(s_raw.at[p], s_raw.at[1 - p], sa_s, sa_r, sibling).wait_recv()
    prepare_s(1 - p)

    for j in (1, 3, 2):
        group = (y + 4 - j) % 4
        for k in range(4):
            slot = group * 4 + (z + 4 - k) % 4
            remote(pf.at[slot, p], pf.at[slot, p], agy_s.at[j, k], agy_r.at[j, k], sibling).wait_recv()
        spread(j)
        to_sibling(j)

    load_pa.wait()
    wide[:, 0:16] = pa_v[...]
    shift = 16 * (yz % 8)
    for k in range(16):
        w = k // 4 + 4 * (k % 4)
        pa_r[64 * k:64 * k + 64, :] = pltpu.roll(wide[64 * w:64 * w + 64, :], shift, 1)

    pc_hi, pc_lo = split(pc[...])
    for j in (2, 1, 3, 0):
        rows = aligned(256 * ((y + j) % 4), 256)
        out1[rows, :] = dot3(s_hi[rows, :], s_lo[rows, :], pc_hi, pc_lo)
        tile = aligned(128 * (y // 2), 128)
        out1[rows, tile] = out1[rows, tile] - pa_r[rows, :]
        if j:
            cp = remote(out1.at[rows], ry.at[j], ry_s.at[j], ry_r.at[j], dev(zl, x, (y + j) % 4, z, p))
            cp.start()
            sends.append(cp)

    for k in range(16):
        high, low = split(pf[k, p])
        p_hi[16 * k:16 * k + 16, :] = high
        p_lo[16 * k:16 * k + 16, :] = low
    for b in (0, 1):
        rows = pl.ds(256 * b, 256)
        out2[rows, :] = dot3(st_hi[rows, :], st_lo[rows, :], p_hi[...], p_lo[...])
    for i, (a, b) in enumerate(row_offsets):
        piece = ((zl + a) % 2) * 4 + (x + b) % 4
        cp = remote(
            out2.at[aligned(64 * piece, 64)], rr.at[i], rr_s.at[i], rr_r.at[i],
            dev((zl + a) % 2, (x + b) % 4, y, z, p),
        )
        cp.start()
        sends.append(cp)

    load_inv.wait()
    for k in range(16):
        for b in (0, 1):
            inv_r[256 * b + 16 * k:256 * b + 16 * k + 16, :] = -inv_v[(2 * k + b) * 16:(2 * k + b) * 16 + 16, :]
    for t in range(4):
        inv_v[128 * t:128 * t + 128, :] = inv_r[:, 128 * t:128 * t + 128].T
    for k in range(16):
        high, low = split(inv_v[aligned((2 * k + p) * 16, 16), :])
        it_hi[16 * k:16 * k + 16, :] = high
        it_lo[16 * k:16 * k + 16, :] = low

    own_piece = aligned(64 * r, 64)
    total = out2[own_piece, :]
    for i in range(7):
        remote(rr.at[i], rr.at[i], rr_s.at[i], rr_r.at[i], sibling).wait_recv()
        total = total + rr[i]
    q_sum[...] = total
    q_zl, q_x = z // 2, 2 * (z % 2) + zl
    stays = jnp.logical_and(jnp.logical_and(q_zl == zl, q_x == x), x == z)
    moves = jnp.logical_not(stays)
    cp_q = remote(q_sum, rq, q_s, q_r, dev(q_zl, q_x, y, x, p))

    @pl.when(moves)
    def _():
        cp_q.start()

    @pl.when(stays)
    def _():
        rq[...] = q_sum[...]

    for j in (1, 3, 2):
        remote(ry.at[j], ry.at[j], ry_s.at[j], ry_r.at[j], sibling).wait_recv()
    for j in (2, 1, 3, 0):
        z2 = (z + j) % 4
        here = aligned(64 * z2, 64)
        t1[here, :] = (
            out1[aligned(256 * y + 64 * z2, 64), :] + ry[1, here, :] + ry[2, here, :] + ry[3, here, :]
        )
        if j:
            cp = remote(t1.at[here], rz.at[j], rz_s.at[j], rz_r.at[j], dev(zl, x, y, z2, p))
            cp.start()
            sends.append(cp)

    for j in range(4):
        group = (y + 4 - j) % 4
        part = pf.at[pl.ds(group * 4, 4), 1 - p]
        remote(part, part, po_s.at[j], po_r.at[j], sibling).wait_recv()
    for k in range(16):
        for b in (0, 1):
            high, low = split(pf[k, b])
            f_hi[32 * k + 16 * b:32 * k + 16 * b + 16, :] = high
            f_lo[32 * k + 16 * b:32 * k + 16 * b + 16, :] = low

    pl.when(moves)(cp_q.wait_recv)
    total = t1[aligned(64 * z, 64), :] + rq[...]
    for j in (1, 3, 2):
        remote(rz.at[j], rz.at[j], rz_s.at[j], rz_r.at[j], sibling).wait_recv()
        total = total + rz[j]
    half = aligned(64 * (z % 2), 64)
    mine = adj.at[half, aligned(256 * p, 256)]
    theirs = adj.at[half, aligned(256 * (1 - p), 256)]
    adj[half, aligned(256 * p, 256)] = total
    cp_f = remote(mine, mine, f_s, f_r, sibling)
    cp_f.start()
    sends.append(cp_f)
    remote(theirs, theirs, f_s, f_r, sibling).wait_recv()

    a_hi, a_lo = split(adj[...])
    gt[...] = dot3(it_hi[...], it_lo[...], a_hi, a_lo)
    gather = []
    for dy in range(4):
        for dz in range(4):
            if dy == 0 and dz == 0:
                continue
            i = dy * 4 + dz
            y2, z2 = (y + dy) % 4, (z + dz) % 4
            cp = remote(
                gt.at[aligned(16 * (y2 * 4 + z2), 16)], rg.at[yz], rg_s.at[i], rg_r.at[i],
                dev(zl, x, y2, z2, p),
            )
            cp.start()
            sends.append(cp)
    rg[yz] = gt[aligned(16 * yz, 16), :]
    for dy in range(4):
        for dz in range(4):
            if dy == 0 and dz == 0:
                continue
            i = dy * 4 + dz
            slot = ((y + 4 - dy) % 4) * 4 + (z + 4 - dz) % 4
            remote(rg.at[slot], rg.at[slot], rg_s.at[i], rg_r.at[i], sibling).wait_recv()
    for t in range(8):
        gfull[:, 128 * t:128 * t + 128] = rg[2 * t] + rg[2 * t + 1]
    grad_ref[...] = gfull[...]

    g_hi, g_lo = split(gfull[...])
    dpart[...] = dot3(g_hi, g_lo, f_hi[...], f_lo[...])
    for i, (a, b) in enumerate(row_offsets):
        cp = remote(
            dpart, rd.at[i], rd_s.at[i], rd_r.at[i], dev((zl + a) % 2, (x + b) % 4, y, z, p)
        )
        cp.start()
        sends.append(cp)
    for i in range(7):
        remote(rd.at[i], rd.at[i], rd_s.at[i], rd_r.at[i], sibling).wait_recv()
    total = jnp.zeros((16, 512), F32)
    for q in range(8):
        a, b = (zl + 2 - q // 4) % 2, (x + 4 - q % 4) % 4
        slot = a * 4 + b
        keep = jnp.where(slot == 0, dpart[...], rd[jnp.maximum(slot - 1, 0)])
        total = total + keep
    diag_row = c * 16 + lax.broadcasted_iota(jnp.int32, (16, 512), 0)
    diag_col = lax.broadcasted_iota(jnp.int32, (16, 512), 1)
    diag_ref[...] = jnp.where(diag_row >= diag_col, -total, 0.0)

    for cp in sends:
        cp.wait_send()
    cp_a.wait_send()
    pl.when(moves)(cp_q.wait_send)
    for cond, cp in conditional:
        pl.when(cond)(cp.wait_send)


def body(adj_trailing, panel, panel_adjoint, inverse_diag):
    vmem, dma = pltpu.VMEM, pltpu.SemaphoreType.DMA
    grad, diag = pl.pallas_call(
        kernel,
        out_shape=(
            jax.ShapeDtypeStruct((16, 1024), F32),
            jax.ShapeDtypeStruct((16, 512), F32),
        ),
        in_specs=[pl.BlockSpec(memory_space=pl.ANY)] * 4,
        out_specs=(pl.BlockSpec(memory_space=vmem), pl.BlockSpec(memory_space=vmem)),
        scratch_shapes=[
            vmem((1024, 16), F32), vmem((1024, 16), F32), vmem((512, 512), F32), vmem((1024, 128), F32),
            vmem((2, 1024, 256), F32), vmem((16, 2, 16, 1024), F32), vmem((256, 512), F32),
            vmem((1024, 512), BF16), vmem((1024, 512), BF16), vmem((512, 1024), BF16), vmem((512, 1024), BF16),
            vmem((256, 1024), BF16), vmem((256, 1024), BF16), vmem((512, 1024), BF16), vmem((512, 1024), BF16),
            vmem((512, 512), F32), vmem((256, 512), BF16), vmem((256, 512), BF16), vmem((1024, 128), F32),
            vmem((1024, 256), F32), vmem((512, 256), F32), vmem((4, 256, 256), F32), vmem((256, 256), F32),
            vmem((4, 64, 256), F32), vmem((7, 64, 256), F32), vmem((64, 256), F32), vmem((64, 256), F32),
            vmem((128, 512), F32), vmem((256, 128), F32), vmem((16, 16, 128), F32), vmem((16, 1024), F32),
            vmem((16, 512), F32), vmem((7, 16, 512), F32),
            dma((4,)), dma((4,)), dma((4,)), dma((4, 4)), dma((4, 4)), dma, dma, dma((2, 4, 3)), dma((2, 4)),
            dma((4,)), dma((4,)), dma((4,)), dma((4,)), dma((7,)), dma((7,)), dma, dma, dma((4,)), dma((4,)),
            dma, dma, dma((16,)), dma((16,)), dma((7,)), dma((7,)),
        ],
        compiler_params=pltpu.CompilerParams(
            collective_id=0, has_side_effects=True, vmem_limit_bytes=48 * 1024 * 1024
        ),
        name="cholesky_step",
    )(adj_trailing, panel, panel_adjoint, inverse_diag)
    grad = jnp.transpose(grad.reshape(16, 4, 4, 64), (2, 1, 3, 0)).reshape(1024, 16)
    return (grad, diag)


def solution(mesh):
    in_specs = (P("row", "col"), P("row", "col"), P("row", "col"), P())
    out_specs = (P("row", "col"), P("col", None))
    return jax.shard_map(body, mesh=mesh, in_specs=in_specs, out_specs=out_specs, check_vma=False)
```

```python
import functools

import jax
import jax.numpy as jnp
from jax import lax
from jax.experimental import pallas as pl
from jax.experimental.pallas import tpu as pltpu
from jax.sharding import PartitionSpec as P

F32 = jnp.float32
BF16 = jnp.bfloat16
MESH = pl.DeviceIdType.MESH
NT = (((1,), (1,)), ((), ()))


def split(value):
    high = value.astype(BF16)
    low = (value - high.astype(F32)).astype(BF16)
    return high, low


def dot3(a_high, a_low, b_high, b_low):
    def one(a, b):
        return lax.dot_general(a, b, NT, preferred_element_type=F32)

    return one(a_high, b_low) + one(a_low, b_high) + one(a_high, b_high)


def aligned(start, size):
    return pl.ds(pl.multiple_of(start, size), size)


def kernel(
    a_hbm, panel_hbm, pa_hbm, inv_hbm, grad_ref, diag_ref,
    panel_v, pa_v, inv_v, wide, s_raw, pf, pc, s_hi, s_lo, st_hi, st_lo,
    p_hi, p_lo, f_hi, f_lo, inv_r, it_hi, it_lo, iq_hi, iq_lo, pa_r, out1, out2, ry, rr,
    qadj, gq, rgq, adj, gt, rg, gfull, dpart, rd,
    local_sem, agz_s, agz_r, agy_s, agy_r, sa_s, sa_r, mini_s, mini_r, pc_s, pc_r, po_s, po_r,
    ry_s, ry_r, rr_s, rr_r, f_s, f_r, rgq_s, rgq_r, rg_s, rg_r, rd_s, rd_r,
):
    r = lax.axis_index("row")
    c = lax.axis_index("col")
    zl, x = r // 4, r % 4
    y, z, p = c // 8, (c // 2) % 4, c % 2
    yz = y * 4 + z

    def dev(zl_, x_, y_, z_, p_):
        return (zl_ * 4 + x_, (y_ * 4 + z_) * 2 + p_)

    def remote(src, dst, send, recv, target):
        return pltpu.make_async_remote_copy(
            src_ref=src, dst_ref=dst, send_sem=send, recv_sem=recv,
            device_id=target, device_id_type=MESH,
        )

    sibling = dev(zl, x, y, z, 1 - p)

    def arrived(ref, send, recv):
        remote(ref, ref, send, recv, sibling).wait_recv()

    barrier = pltpu.get_barrier_semaphore()
    greet = [sibling]
    greet += [dev(zl, x, y, (z + j) % 4, p) for j in (1, 2, 3)]
    greet += [dev(zl, x, (y + j) % 4, z, p) for j in (1, 2, 3)]
    row_offsets = [(a, b) for a in (0, 1) for b in (0, 1, 2, 3) if (a, b) != (0, 0)]
    greet += [dev((zl + a) % 2, (x + b) % 4, y, z, p) for a, b in row_offsets]
    for target in greet:
        pl.semaphore_signal(barrier, inc=1, device_id=target, device_id_type=MESH)
    to_row, to_z = yz // 2, r // 2
    keeps = jnp.logical_and(to_row == r, to_z == z)
    for b in (0, 1):
        for h in (0, 1):
            is_me = jnp.logical_and(keeps, jnp.logical_and(r % 2 == b, z % 2 == h))

            @pl.when(jnp.logical_not(is_me))
            def _():
                pl.semaphore_signal(
                    barrier, inc=1, device_id=(2 * z + b, ((r // 2) * 4 + (r % 2) * 2 + h) * 2 + p),
                    device_id_type=MESH,
                )

    load_panel = pltpu.make_async_copy(panel_hbm, panel_v, local_sem.at[0])
    load_a = pltpu.make_async_copy(a_hbm, s_raw.at[p], local_sem.at[1])
    load_pa = pltpu.make_async_copy(pa_hbm, pa_v, local_sem.at[2])
    load_inv = pltpu.make_async_copy(inv_hbm, inv_v, local_sem.at[3])
    load_panel.start()
    load_a.start()
    load_pa.start()
    load_inv.start()

    left = lax.broadcasted_iota(jnp.int32, (16, 128), 1) < 64

    def ordered(ref, t):
        w1 = t // 2 + 8 * (t % 2)
        one = ref[:, 128 * (w1 // 2):128 * (w1 // 2) + 128]
        two = ref[:, 128 * (w1 // 2 + 2):128 * (w1 // 2 + 2) + 128]
        if w1 % 2:
            one = pltpu.roll(one, 64, 1)
        else:
            two = pltpu.roll(two, 64, 1)
        return jnp.where(left, one, two)

    load_panel.wait()
    for t in range(8):
        pf[yz, p, :, 128 * t:128 * t + 128] = ordered(panel_v, t)

    pl.semaphore_wait(barrier, len(greet) + 3 + jnp.where(keeps, 0, 1))

    sends = []
    conditional = []

    for j in (1, 3, 2, 0):
        y2 = (y + j) % 4
        src = pf.at[yz, p, :, aligned(256 * y2, 256)]
        dst = pc.at[aligned(16 * yz, 16), aligned(256 * (r % 2), 256)]
        cp = remote(src, dst, mini_s.at[j], mini_r.at[r % 2, z % 2], (to_row, (y2 * 4 + to_z) * 2 + p))
        if j:
            cp.start()
            sends.append(cp)
        else:
            pl.when(jnp.logical_not(keeps))(cp.start)
            conditional.append((jnp.logical_not(keeps), cp))

    @pl.when(keeps)
    def _():
        pc[aligned(16 * yz, 16), aligned(256 * (r % 2), 256)] = pf[yz, p, :, aligned(256 * y, 256)]

    for j in (1, 3, 2):
        cp = remote(pf.at[yz, p], pf.at[yz, p], agz_s.at[j], agz_r.at[j], dev(zl, x, y, (z + j) % 4, p))
        cp.start()
        sends.append(cp)

    def forward_y(k):
        slot = y * 4 + (z + 4 - k) % 4
        for j in (1, 3, 2):
            cp = remote(
                pf.at[slot, p], pf.at[slot, p], agy_s.at[j, k], agy_r.at[j, k],
                dev(zl, x, (y + j) % 4, z, p),
            )
            cp.start()
            sends.append(cp)

    forward_y(0)
    load_a.wait()
    cp_a = remote(s_raw.at[p], s_raw.at[p], sa_s, sa_r, sibling)
    cp_a.start()
    sends.append(cp_a)

    lane = lax.broadcasted_iota(jnp.int32, (128, 256), 1)
    line = lax.broadcasted_iota(jnp.int32, (128, 256), 0)

    def col_nat(b):
        return (32 * (lane // 64) + c - p + b) * 64 + lane % 64

    def prepare(b):
        cols = (32 * (lane // 64) + c - p + b) * 64 + lane % 64

        def step(t, carry):
            w1 = t // 2 + 8 * (t % 2)
            rows = jnp.concatenate(
                [s_raw[b, aligned(64 * w1, 64), :], s_raw[b, aligned(64 * w1 + 256, 64), :]], axis=0
            )
            row_nat = (8 * w1 + r) * 64 + line + jnp.where(line >= 64, 32 * 64 - 64, 0)
            value = jnp.where(row_nat >= cols, rows, 0.0)
            high, low = split(value)
            s_hi[aligned(128 * t, 128), aligned(256 * b, 256)] = high
            s_lo[aligned(128 * t, 128), aligned(256 * b, 256)] = low
            high, low = split(value.T)
            st_hi[aligned(256 * b, 256), aligned(128 * t, 128)] = high
            st_lo[aligned(256 * b, 256), aligned(128 * t, 128)] = low
            return carry

        lax.fori_loop(0, 8, step, 0)

    load_pa.wait()
    wide[...] = jnp.zeros_like(wide)
    for t in range(8):
        wide[aligned(16 * (yz % 8), 16), 128 * t:128 * t + 128] = ordered(pa_v, t)
    for t in range(8):
        pa_r[128 * t:128 * t + 128, :] = wide[:, 128 * t:128 * t + 128].T

    for k in (1, 3, 2):
        arrived(pf.at[0, 0], agz_s.at[k], agz_r.at[k])
        forward_y(k)

    for b in (0, 1):
        for h in (0, 1):
            is_me = jnp.logical_and(keeps, jnp.logical_and(r % 2 == b, z % 2 == h))

            @pl.when(jnp.logical_not(is_me))
            def _():
                arrived(pc.at[0:16, 0:256], mini_s.at[0], mini_r.at[b, h])

    def pass_x(zl_, k):
        part = pc.at[aligned(32 * (4 * zl_ + x), 32)]
        for j in (1, 3, 2):
            cp = remote(part, part, pc_s.at[k, j], pc_r.at[k, j], dev(zl, (x + j) % 4, y, z, p))
            cp.start()
            sends.append(cp)

    part = pc.at[aligned(32 * r, 32)]
    cp = remote(part, part, pc_s.at[0, 0], pc_r.at[0, 0], dev(1 - zl, x, y, z, p))
    cp.start()
    sends.append(cp)
    pass_x(zl, 0)
    arrived(pc.at[0:32], pc_s.at[0, 0], pc_r.at[0, 0])
    pass_x(1 - zl, 1)
    prepare(p)
    arrived(s_raw.at[0], sa_s, sa_r)
    prepare(1 - p)
    for k in (0, 1):
        for j in (1, 3, 2):
            arrived(pc.at[0:32], pc_s.at[k, j], pc_r.at[k, j])

    pc_hi, pc_lo = split(pc[...])
    tile = aligned(128 * (y // 2), 128)
    for h in (0, 1):
        for j in (1, 3, 2, 0):
            rows = aligned(256 * ((y + j) % 4) + 128 * h, 128)
            out1[rows, :] = dot3(s_hi[rows, :], s_lo[rows, :], pc_hi, pc_lo)
            out1[rows, tile] = out1[rows, tile] - pa_r[rows, :]
            if j:
                cp = remote(
                    out1.at[rows], ry.at[j, h], ry_s.at[j, h], ry_r.at[j, h], dev(zl, x, (y + j) % 4, z, p)
                )
                cp.start()
                sends.append(cp)

    for j in (1, 3, 2):
        for k in range(4):
            arrived(pf.at[0, 0], agy_s.at[j, k], agy_r.at[j, k])
    cp = remote(pf.at[:, p], pf.at[:, p], po_s, po_r, sibling)
    cp.start()
    sends.append(cp)
    for k in range(16):
        high, low = split(pf[k, p])
        p_hi[16 * k:16 * k + 16, :] = high
        p_lo[16 * k:16 * k + 16, :] = low
    for b in (0, 1):
        rows = pl.ds(256 * b, 256)
        out2[rows, :] = dot3(st_hi[rows, :], st_lo[rows, :], p_hi[...], p_lo[...])
    for i, (a, b) in enumerate(row_offsets):
        piece = ((zl + a) % 2) * 4 + (x + b) % 4
        cp = remote(
            out2.at[aligned(64 * piece, 64)], rr.at[i], rr_s.at[i], rr_r.at[i],
            dev((zl + a) % 2, (x + b) % 4, y, z, p),
        )
        cp.start()
        sends.append(cp)

    load_inv.wait()
    for k in range(16):
        for b in (0, 1):
            inv_r[256 * b + 16 * k:256 * b + 16 * k + 16, :] = -inv_v[(2 * k + b) * 16:(2 * k + b) * 16 + 16, :]
    for t in range(4):
        inv_v[128 * t:128 * t + 128, :] = inv_r[:, 128 * t:128 * t + 128].T
    for k in range(16):
        high, low = split(inv_v[aligned((2 * k + p) * 16, 16), :])
        it_hi[16 * k:16 * k + 16, :] = high
        it_lo[16 * k:16 * k + 16, :] = low

    for k in range(8):
        for e in (0, 1):
            first = inv_v[aligned((4 * k + p) * 16 + 8 * e, 8), :]
            second = inv_v[aligned((4 * k + 2 + p) * 16 + 8 * e, 8), :]
            high, low = split(jnp.concatenate([first, second], axis=0))
            iq_hi[e, 16 * k:16 * k + 16, :] = high
            iq_lo[e, 16 * k:16 * k + 16, :] = low

    own = aligned(256 * p, 256)
    offsets = [(dy, dz) for dz in (2, 1, 3, 0) for dy in (2, 1, 3, 0)]
    others = offsets[:-1]

    def swap(ref, k):
        cp = remote(ref, ref, f_s.at[k], f_r.at[k], sibling)
        cp.start()
        sends.append(cp)

    def sum_y(h):
        for j in (1, 3, 2):
            arrived(ry.at[0, 0], ry_s.at[j, h], ry_r.at[j, h])
        adj[h, :, own] = (
            out1[aligned(256 * y + 128 * h, 128), :] + ry[1, h] + ry[2, h] + ry[3, h]
        )
        swap(adj.at[h, :, own], h)

    def to_owners(h):
        arrived(adj.at[h, :, 0:256], f_s.at[h], f_r.at[h])
        a_hi, a_lo = split(adj[h])
        gt[h] = dot3(it_hi[...], it_lo[...], a_hi, a_lo)
        for dy, dz in others:
            i = dy * 4 + dz
            y2, z2 = (y + dy) % 4, (z + dz) % 4
            cp = remote(
                gt.at[h, aligned(16 * (y2 * 4 + z2), 16)], rg.at[h, yz], rg_s.at[h, i], rg_r.at[h, i],
                dev(zl, x, y2, z2, p),
            )
            cp.start()
            sends.append(cp)
        rg[h, yz] = gt[h, aligned(16 * yz, 16), :]

    sum_y(0)
    to_owners(0)

    total = out2[aligned(64 * r, 64), :]
    for i in range(7):
        arrived(rr.at[i], rr_s.at[i], rr_r.at[i])
        total = total + rr[i]
    qadj[:, own] = total
    swap(qadj.at[:, own], 2)
    sum_y(1)

    arrived(qadj.at[:, 0:256], f_s.at[2], f_r.at[2])
    a_hi, a_lo = split(qadj[...])
    none = jnp.zeros((64, 512), BF16)
    gq[...] = dot3(
        iq_hi[0], iq_lo[0], jnp.concatenate([a_hi, none], axis=0), jnp.concatenate([a_lo, none], axis=0)
    ) + dot3(
        iq_hi[1], iq_lo[1], jnp.concatenate([none, a_hi], axis=0), jnp.concatenate([none, a_lo], axis=0)
    )
    q_row, q_slot = 2 * z + zl, y * 4 + x
    stays = q_row == r
    moves = jnp.logical_not(stays)
    for dy, dz in offsets:
        i = dy * 4 + dz
        to = ((y + dy) % 4) * 4 + (z + dz) % 4
        cp = remote(
            gq.at[aligned(8 * to, 8)], rgq.at[q_slot], rgq_s.at[i], rgq_r.at[q_slot], (q_row, to * 2 + p)
        )
        if i:
            cp.start()
            sends.append(cp)
        else:
            pl.when(moves)(cp.start)
            conditional.append((moves, cp))

    @pl.when(stays)
    def _():
        rgq[q_slot] = gq[aligned(8 * yz, 8), :]

    to_owners(1)

    arrived(pf.at[:, 0], po_s, po_r)
    for k in range(16):
        for b in (0, 1):
            high, low = split(pf[k, b])
            f_hi[32 * k + 16 * b:32 * k + 16 * b + 16, :] = high
            f_lo[32 * k + 16 * b:32 * k + 16 * b + 16, :] = low

    for h in (0, 1):
        for dy, dz in others:
            i = dy * 4 + dz
            arrived(rg.at[0, 0], rg_s.at[h, i], rg_r.at[h, i])
    for slot in range(16):
        @pl.when(jnp.logical_not(jnp.logical_and(stays, q_slot == slot)))
        def _():
            arrived(rgq.at[0], rgq_s.at[0], rgq_r.at[slot])

    low_half = left[0:8]
    for t in range(8):
        h, g = t % 2, 4 * (t // 2)
        parts = (rg[h, g] + rg[h, g + 1]) + (rg[h, g + 2] + rg[h, g + 3])
        one, two = rgq[2 * t], rgq[2 * t + 1]
        upper = jnp.where(low_half, one, pltpu.roll(two, 64, 1))
        lower = jnp.where(low_half, pltpu.roll(one, 64, 1), two)
        gfull[:, 128 * t:128 * t + 128] = parts + jnp.concatenate([upper, lower], axis=0)

    g_hi, g_lo = split(gfull[...])
    dpart[...] = dot3(g_hi, g_lo, f_hi[...], f_lo[...])
    for i, (a, b) in enumerate(row_offsets):
        cp = remote(
            dpart, rd.at[i], rd_s.at[i], rd_r.at[i], dev((zl + a) % 2, (x + b) % 4, y, z, p)
        )
        cp.start()
        sends.append(cp)
    for t in range(8):
        w = 2 * t
        k1 = (w % 4) * 4 + w // 4
        k2 = k1 + 4
        one = gfull[:, 128 * (k1 // 2):128 * (k1 // 2) + 128]
        two = gfull[:, 128 * (k2 // 2):128 * (k2 // 2) + 128]
        if k1 % 2:
            one = pltpu.roll(one, 64, 1)
        else:
            two = pltpu.roll(two, 64, 1)
        grad_ref[:, 128 * t:128 * t + 128] = jnp.where(left, one, two)
    for i in range(7):
        arrived(rd.at[i], rd_s.at[i], rd_r.at[i])
    total = jnp.zeros((16, 512), F32)
    for q in range(8):
        a, b = (zl + 2 - q // 4) % 2, (x + 4 - q % 4) % 4
        slot = a * 4 + b
        keep = jnp.where(slot == 0, dpart[...], rd[jnp.maximum(slot - 1, 0)])
        total = total + keep
    diag_row = c * 16 + lax.broadcasted_iota(jnp.int32, (16, 512), 0)
    diag_col = lax.broadcasted_iota(jnp.int32, (16, 512), 1)
    diag_ref[...] = jnp.where(diag_row >= diag_col, -total, 0.0)

    for cp in sends:
        cp.wait_send()
    for cond, cp in conditional:
        pl.when(cond)(cp.wait_send)


def body(adj_trailing, panel, panel_adjoint, inverse_diag):
    vmem, dma = pltpu.VMEM, pltpu.SemaphoreType.DMA
    operands = (adj_trailing, panel.T, panel_adjoint.T, inverse_diag)
    grad, diag = pl.pallas_call(
        kernel,
        out_shape=(
            jax.ShapeDtypeStruct((16, 1024), F32),
            jax.ShapeDtypeStruct((16, 512), F32),
        ),
        in_specs=[pl.BlockSpec(memory_space=pl.ANY)] * 4,
        out_specs=(pl.BlockSpec(memory_space=vmem), pl.BlockSpec(memory_space=vmem)),
        scratch_shapes=[
            vmem((16, 1024), F32), vmem((16, 1024), F32), vmem((512, 512), F32), vmem((128, 1024), F32),
            vmem((2, 1024, 256), F32), vmem((16, 2, 16, 1024), F32), vmem((256, 512), F32),
            vmem((1024, 512), BF16), vmem((1024, 512), BF16), vmem((512, 1024), BF16), vmem((512, 1024), BF16),
            vmem((256, 1024), BF16), vmem((256, 1024), BF16), vmem((512, 1024), BF16), vmem((512, 1024), BF16),
            vmem((512, 512), F32), vmem((256, 512), BF16), vmem((256, 512), BF16),
            vmem((2, 128, 512), BF16), vmem((2, 128, 512), BF16), vmem((1024, 128), F32),
            vmem((1024, 256), F32), vmem((512, 256), F32), vmem((4, 2, 128, 256), F32), vmem((7, 64, 256), F32),
            vmem((64, 512), F32), vmem((128, 128), F32), vmem((16, 8, 128), F32),
            vmem((2, 128, 512), F32), vmem((2, 256, 128), F32), vmem((2, 16, 16, 128), F32), vmem((16, 1024), F32),
            vmem((16, 512), F32), vmem((7, 16, 512), F32),
            dma((4,)), dma((4,)), dma((4,)), dma((4, 4)), dma((4, 4)), dma, dma, dma((4,)), dma((2, 2)),
            dma((2, 4)), dma((2, 4)), dma, dma,
            dma((4, 2)), dma((4, 2)), dma((7,)), dma((7,)), dma((3,)), dma((3,)), dma((16,)), dma((16,)),
            dma((2, 16)), dma((2, 16)), dma((7,)), dma((7,)),
        ],
        compiler_params=pltpu.CompilerParams(
            collective_id=0, has_side_effects=True, vmem_limit_bytes=40 * 1024 * 1024
        ),
        name="cholesky_step",
    )(*(pltpu.with_memory_space_constraint(a, pltpu.HBM) for a in operands))
    return (grad.T, diag)


def solution(mesh):
    in_specs = (P("row", "col"), P("row", "col"), P("row", "col"), P())
    out_specs = (P("row", "col"), P("col", None))
    return jax.shard_map(body, mesh=mesh, in_specs=in_specs, out_specs=out_specs, check_vma=False)
```

```python
import functools

import jax
import jax.numpy as jnp
from jax import lax
from jax.experimental import pallas as pl
from jax.experimental.pallas import tpu as pltpu
from jax.sharding import PartitionSpec as P

F32 = jnp.float32
BF16 = jnp.bfloat16
MESH = pl.DeviceIdType.MESH
NT = (((1,), (1,)), ((), ()))


def split(value):
    high = value.astype(BF16)
    low = (value - high.astype(F32)).astype(BF16)
    return high, low


def dot3(a_high, a_low, b_high, b_low):
    def one(a, b):
        return lax.dot_general(a, b, NT, preferred_element_type=F32)

    return one(a_high, b_low) + one(a_low, b_high) + one(a_high, b_high)


def aligned(start, size):
    return pl.ds(pl.multiple_of(start, size), size)


def kernel(
    a_hbm, panel_hbm, pa_hbm, inv_hbm, grad_ref, diag_ref,
    panel_v, pa_v, inv_v, wide, s_raw, pf, pc, s_hi, s_lo, st_hi, st_lo,
    p_hi, p_lo, f_hi, f_lo, inv_r, it_hi, it_lo, iq_hi, iq_lo, pa_r, out1, out2, ry, rr,
    qadj, gq, rgq, adj, gt, rg, gfull, dpart, rd,
    local_sem, agz_s, agz_r, agy_s, agy_r, sa_s, sa_r, mini_s, mini_r, pc_s, pc_r, po_s, po_r,
    ry_s, ry_r, rr_s, rr_r, f_s, f_r, rgq_s, rgq_r, rg_s, rg_r, rd_s, rd_r,
):
    r = lax.axis_index("row")
    c = lax.axis_index("col")
    zl, x = r // 4, r % 4
    y, z, p = c // 8, (c // 2) % 4, c % 2
    yz = y * 4 + z

    def dev(zl_, x_, y_, z_, p_):
        return (zl_ * 4 + x_, (y_ * 4 + z_) * 2 + p_)

    def remote(src, dst, send, recv, target):
        return pltpu.make_async_remote_copy(
            src_ref=src, dst_ref=dst, send_sem=send, recv_sem=recv,
            device_id=target, device_id_type=MESH,
        )

    sibling = dev(zl, x, y, z, 1 - p)

    def arrived(ref, send, recv):
        remote(ref, ref, send, recv, sibling).wait_recv()

    barrier = pltpu.get_barrier_semaphore()
    greet = [sibling]
    greet += [dev(zl, x, y, (z + j) % 4, p) for j in (1, 2, 3)]
    greet += [dev(zl, x, (y + j) % 4, z, p) for j in (1, 2, 3)]
    row_offsets = [(a, b) for a in (0, 1) for b in (0, 1, 2, 3) if (a, b) != (0, 0)]
    greet += [dev((zl + a) % 2, (x + b) % 4, y, z, p) for a, b in row_offsets]
    for target in greet:
        pl.semaphore_signal(barrier, inc=1, device_id=target, device_id_type=MESH)
    to_row, to_z = (z // 2) * 4 + y, r // 2
    keeps = jnp.logical_and(to_row == r, to_z == z)
    for b in (0, 1):
        for h in (0, 1):
            is_me = jnp.logical_and(keeps, jnp.logical_and(r % 2 == b, z % 2 == h))

            @pl.when(jnp.logical_not(is_me))
            def _():
                pl.semaphore_signal(
                    barrier, inc=1, device_id=(2 * z + b, (x * 4 + zl * 2 + h) * 2 + p),
                    device_id_type=MESH,
                )

    load_panel = pltpu.make_async_copy(panel_hbm, panel_v, local_sem.at[0])
    load_a = pltpu.make_async_copy(a_hbm, s_raw.at[p], local_sem.at[1])
    load_pa = pltpu.make_async_copy(pa_hbm, pa_v, local_sem.at[2])
    load_inv = pltpu.make_async_copy(inv_hbm, inv_v, local_sem.at[3])
    load_panel.start()
    load_a.start()
    load_pa.start()
    load_inv.start()

    left = lax.broadcasted_iota(jnp.int32, (16, 128), 1) < 64

    def ordered(ref, t):
        w1 = t // 2 + 8 * (t % 2)
        one = ref[:, 128 * (w1 // 2):128 * (w1 // 2) + 128]
        two = ref[:, 128 * (w1 // 2 + 2):128 * (w1 // 2 + 2) + 128]
        if w1 % 2:
            one = pltpu.roll(one, 64, 1)
        else:
            two = pltpu.roll(two, 64, 1)
        return jnp.where(left, one, two)

    load_panel.wait()
    for t in range(8):
        pf[yz, p, :, 128 * t:128 * t + 128] = ordered(panel_v, t)

    pl.semaphore_wait(barrier, len(greet) + 3 + jnp.where(keeps, 0, 1))

    sends = []
    conditional = []

    def drain():
        while sends:
            sends.pop().wait_send()
        while conditional:
            cond, cp = conditional.pop()
            pl.when(cond)(cp.wait_send)


    for j in (1, 3, 2, 0):
        y2 = (y + j) % 4
        src = pf.at[yz, p, :, aligned(256 * y2, 256)]
        dst = pc.at[aligned(16 * yz, 16), aligned(256 * (r % 2), 256)]
        cp = remote(src, dst, mini_s.at[j], mini_r.at[r % 2, z % 2], (to_row, (y2 * 4 + to_z) * 2 + p))
        if j:
            cp.start()
            sends.append(cp)
        else:
            pl.when(jnp.logical_not(keeps))(cp.start)
            conditional.append((jnp.logical_not(keeps), cp))

    @pl.when(keeps)
    def _():
        pc[aligned(16 * yz, 16), aligned(256 * (r % 2), 256)] = pf[yz, p, :, aligned(256 * y, 256)]

    for j in (1, 3, 2):
        cp = remote(pf.at[yz, p], pf.at[yz, p], agz_s.at[j], agz_r.at[j], dev(zl, x, y, (z + j) % 4, p))
        cp.start()
        sends.append(cp)

    def forward_y(k):
        slot = y * 4 + (z + 4 - k) % 4
        for j in (1, 3, 2):
            cp = remote(
                pf.at[slot, p], pf.at[slot, p], agy_s.at[j, k], agy_r.at[j, k],
                dev(zl, x, (y + j) % 4, z, p),
            )
            cp.start()
            sends.append(cp)

    forward_y(0)
    load_a.wait()
    cp_a = remote(s_raw.at[p], s_raw.at[p], sa_s, sa_r, sibling)
    cp_a.start()
    sends.append(cp_a)

    lane = lax.broadcasted_iota(jnp.int32, (128, 256), 1)
    line = lax.broadcasted_iota(jnp.int32, (128, 256), 0)

    def col_nat(b):
        return (32 * (lane // 64) + c - p + b) * 64 + lane % 64

    def prepare(b):
        cols = (32 * (lane // 64) + c - p + b) * 64 + lane % 64

        def step(t, carry):
            w1 = t // 2 + 8 * (t % 2)
            rows = jnp.concatenate(
                [s_raw[b, aligned(64 * w1, 64), :], s_raw[b, aligned(64 * w1 + 256, 64), :]], axis=0
            )
            row_nat = (8 * w1 + r) * 64 + line + jnp.where(line >= 64, 32 * 64 - 64, 0)
            value = jnp.where(row_nat >= cols, rows, 0.0)
            high, low = split(value)
            s_hi[aligned(128 * t, 128), aligned(256 * b, 256)] = high
            s_lo[aligned(128 * t, 128), aligned(256 * b, 256)] = low
            high, low = split(value.T)
            st_hi[aligned(256 * b, 256), aligned(128 * t, 128)] = high
            st_lo[aligned(256 * b, 256), aligned(128 * t, 128)] = low
            return carry

        lax.fori_loop(0, 8, step, 0)

    for k in (1, 3, 2):
        arrived(pf.at[0, 0], agz_s.at[k], agz_r.at[k])
        forward_y(k)

    for b in (0, 1):
        for h in (0, 1):
            is_me = jnp.logical_and(keeps, jnp.logical_and(r % 2 == b, z % 2 == h))

            @pl.when(jnp.logical_not(is_me))
            def _():
                arrived(pc.at[0:16, 0:256], mini_s.at[0], mini_r.at[b, h])

    part = pc.at[aligned(32 * (2 * x + zl), 32)]
    for a, b in ((1, 2), (1, 1), (1, 3), (1, 0), (0, 2), (0, 1), (0, 3)):
        cp = remote(part, part, pc_s.at[a, b], pc_r.at[a, b], dev((zl + a) % 2, (x + b) % 4, y, z, p))
        cp.start()
        sends.append(cp)
    prepare(p)
    load_pa.wait()
    wide[...] = jnp.zeros_like(wide)
    for t in range(8):
        wide[aligned(16 * (yz % 8), 16), 128 * t:128 * t + 128] = ordered(pa_v, t)
    for t in range(8):
        pa_r[128 * t:128 * t + 128, :] = wide[:, 128 * t:128 * t + 128].T

    arrived(s_raw.at[0], sa_s, sa_r)
    prepare(1 - p)
    for a, b in row_offsets:
        arrived(pc.at[0:32], pc_s.at[a, b], pc_r.at[a, b])

    pc_hi, pc_lo = split(pc[...])
    tile = aligned(128 * (y // 2), 128)
    for h, j in ((0, 1), (0, 3), (0, 2), (1, 1), (1, 3), (1, 2), (0, 0), (1, 0)):
        rows = aligned(256 * ((y + j) % 4) + 128 * h, 128)
        out1[rows, :] = dot3(s_hi[rows, :], s_lo[rows, :], pc_hi, pc_lo)
        out1[rows, tile] = out1[rows, tile] - pa_r[rows, :]
        if j:
            cp = remote(
                out1.at[rows], ry.at[j, h], ry_s.at[j, h], ry_r.at[j, h], dev(zl, x, (y + j) % 4, z, p)
            )
            cp.start()
            sends.append(cp)

    for j in (1, 3, 2):
        for k in range(4):
            arrived(pf.at[0, 0], agy_s.at[j, k], agy_r.at[j, k])
    cp = remote(pf.at[:, p], pf.at[:, p], po_s, po_r, sibling)
    cp.start()
    sends.append(cp)
    for k in range(16):
        high, low = split(pf[k, p])
        p_hi[16 * k:16 * k + 16, :] = high
        p_lo[16 * k:16 * k + 16, :] = low
    for b in (0, 1):
        rows = pl.ds(256 * b, 256)
        out2[rows, :] = dot3(st_hi[rows, :], st_lo[rows, :], p_hi[...], p_lo[...])
    for i, (a, b) in enumerate(row_offsets):
        piece = ((zl + a) % 2) * 4 + (x + b) % 4
        cp = remote(
            out2.at[aligned(64 * piece, 64)], rr.at[i], rr_s.at[i], rr_r.at[i],
            dev((zl + a) % 2, (x + b) % 4, y, z, p),
        )
        cp.start()
        sends.append(cp)

    load_inv.wait()
    for k in range(16):
        for b in (0, 1):
            inv_r[256 * b + 16 * k:256 * b + 16 * k + 16, :] = -inv_v[(2 * k + b) * 16:(2 * k + b) * 16 + 16, :]
    for t in range(4):
        inv_v[128 * t:128 * t + 128, :] = inv_r[:, 128 * t:128 * t + 128].T
    for k in range(16):
        high, low = split(inv_v[aligned((2 * k + p) * 16, 16), :])
        it_hi[16 * k:16 * k + 16, :] = high
        it_lo[16 * k:16 * k + 16, :] = low

    for k in range(8):
        for e in (0, 1):
            first = inv_v[aligned((4 * k + p) * 16 + 8 * e, 8), :]
            second = inv_v[aligned((4 * k + 2 + p) * 16 + 8 * e, 8), :]
            high, low = split(jnp.concatenate([first, second], axis=0))
            iq_hi[e, 16 * k:16 * k + 16, :] = high
            iq_lo[e, 16 * k:16 * k + 16, :] = low

    own = aligned(256 * p, 256)
    offsets = [(dy, dz) for dz in (2, 1, 3, 0) for dy in (2, 1, 3, 0)]
    others = offsets[:-1]

    def swap(ref, k):
        cp = remote(ref, ref, f_s.at[k], f_r.at[k], sibling)
        cp.start()
        sends.append(cp)

    def sum_y(h):
        for j in (1, 3, 2):
            arrived(ry.at[0, 0], ry_s.at[j, h], ry_r.at[j, h])
        adj[h, :, own] = (
            out1[aligned(256 * y + 128 * h, 128), :] + ry[1, h] + ry[2, h] + ry[3, h]
        )
        swap(adj.at[h, :, own], h)

    def to_owners(h):
        arrived(adj.at[h, :, 0:256], f_s.at[h], f_r.at[h])
        a_hi, a_lo = split(adj[h])
        gt[h] = dot3(it_hi[...], it_lo[...], a_hi, a_lo)
        for dy, dz in others:
            i = dy * 4 + dz
            y2, z2 = (y + dy) % 4, (z + dz) % 4
            cp = remote(
                gt.at[h, aligned(16 * (y2 * 4 + z2), 16)], rg.at[h, yz], rg_s.at[h, i], rg_r.at[h, i],
                dev(zl, x, y2, z2, p),
            )
            cp.start()
            sends.append(cp)
        rg[h, yz] = gt[h, aligned(16 * yz, 16), :]

    sum_y(0)
    to_owners(0)

    total = out2[aligned(64 * r, 64), :]
    for i in range(7):
        arrived(rr.at[i], rr_s.at[i], rr_r.at[i])
        total = total + rr[i]
    qadj[:, own] = total
    swap(qadj.at[:, own], 2)
    sum_y(1)

    arrived(qadj.at[:, 0:256], f_s.at[2], f_r.at[2])
    a_hi, a_lo = split(qadj[...])
    none = jnp.zeros((64, 512), BF16)
    gq[...] = dot3(
        iq_hi[0], iq_lo[0], jnp.concatenate([a_hi, none], axis=0), jnp.concatenate([a_lo, none], axis=0)
    ) + dot3(
        iq_hi[1], iq_lo[1], jnp.concatenate([none, a_hi], axis=0), jnp.concatenate([none, a_lo], axis=0)
    )
    q_row, q_slot = 2 * z + zl, y * 4 + x
    stays = q_row == r
    moves = jnp.logical_not(stays)
    for dy, dz in offsets:
        i = dy * 4 + dz
        to = ((y + dy) % 4) * 4 + (z + dz) % 4
        cp = remote(
            gq.at[aligned(8 * to, 8)], rgq.at[q_slot], rgq_s.at[i], rgq_r.at[q_slot], (q_row, to * 2 + p)
        )
        if i:
            cp.start()
            sends.append(cp)
        else:
            pl.when(moves)(cp.start)
            conditional.append((moves, cp))

    @pl.when(stays)
    def _():
        rgq[q_slot] = gq[aligned(8 * yz, 8), :]

    to_owners(1)

    arrived(pf.at[:, 0], po_s, po_r)
    for k in range(16):
        for b in (0, 1):
            high, low = split(pf[k, b])
            f_hi[32 * k + 16 * b:32 * k + 16 * b + 16, :] = high
            f_lo[32 * k + 16 * b:32 * k + 16 * b + 16, :] = low

    drain()
    for h in (0, 1):
        for dy, dz in others:
            i = dy * 4 + dz
            arrived(rg.at[0, 0], rg_s.at[h, i], rg_r.at[h, i])
    for slot in range(16):
        @pl.when(jnp.logical_not(jnp.logical_and(stays, q_slot == slot)))
        def _():
            arrived(rgq.at[0], rgq_s.at[0], rgq_r.at[slot])

    low_half = left[0:8]
    for t in range(8):
        h, g = t % 2, 4 * (t // 2)
        parts = (rg[h, g] + rg[h, g + 1]) + (rg[h, g + 2] + rg[h, g + 3])
        one, two = rgq[2 * t], rgq[2 * t + 1]
        upper = jnp.where(low_half, one, pltpu.roll(two, 64, 1))
        lower = jnp.where(low_half, pltpu.roll(one, 64, 1), two)
        gfull[:, 128 * t:128 * t + 128] = parts + jnp.concatenate([upper, lower], axis=0)

    g_hi, g_lo = split(gfull[...])
    both = lax.dot_general(
        jnp.concatenate([g_hi, g_lo], axis=0), f_hi[...], NT, preferred_element_type=F32
    )
    cross = lax.dot_general(g_hi, f_lo[...], NT, preferred_element_type=F32)
    dpart[...] = both[0:16, :] + (both[16:32, :] + cross)
    for a, b in ((1, 2), (0, 2), (1, 1), (1, 3), (1, 0), (0, 1), (0, 3)):
        i = a * 4 + b - 1
        cp = remote(
            dpart, rd.at[i], rd_s.at[i], rd_r.at[i], dev((zl + a) % 2, (x + b) % 4, y, z, p)
        )
        cp.start()
        sends.append(cp)
    for t in range(8):
        w = 2 * t
        k1 = (w % 4) * 4 + w // 4
        k2 = k1 + 4
        one = gfull[:, 128 * (k1 // 2):128 * (k1 // 2) + 128]
        two = gfull[:, 128 * (k2 // 2):128 * (k2 // 2) + 128]
        if k1 % 2:
            one = pltpu.roll(one, 64, 1)
        else:
            two = pltpu.roll(two, 64, 1)
        grad_ref[:, 128 * t:128 * t + 128] = jnp.where(left, one, two)
    for i in range(7):
        arrived(rd.at[i], rd_s.at[i], rd_r.at[i])
    total = jnp.zeros((16, 512), F32)
    for q in range(8):
        a, b = (zl + 2 - q // 4) % 2, (x + 4 - q % 4) % 4
        slot = a * 4 + b
        keep = jnp.where(slot == 0, dpart[...], rd[jnp.maximum(slot - 1, 0)])
        total = total + keep
    diag_row = c * 16 + lax.broadcasted_iota(jnp.int32, (16, 512), 0)
    diag_col = lax.broadcasted_iota(jnp.int32, (16, 512), 1)
    diag_ref[...] = jnp.where(diag_row >= diag_col, -total, 0.0)

    drain()


def body(adj_trailing, panel, panel_adjoint, inverse_diag):
    vmem, dma = pltpu.VMEM, pltpu.SemaphoreType.DMA
    operands = (adj_trailing, panel.T, panel_adjoint.T, inverse_diag)
    grad, diag = pl.pallas_call(
        kernel,
        out_shape=(
            jax.ShapeDtypeStruct((16, 1024), F32),
            jax.ShapeDtypeStruct((16, 512), F32),
        ),
        in_specs=[pl.BlockSpec(memory_space=pl.ANY)] * 4,
        out_specs=(pl.BlockSpec(memory_space=vmem), pl.BlockSpec(memory_space=vmem)),
        scratch_shapes=[
            vmem((16, 1024), F32), vmem((16, 1024), F32), vmem((512, 512), F32), vmem((128, 1024), F32),
            vmem((2, 1024, 256), F32), vmem((16, 2, 16, 1024), F32), vmem((256, 512), F32),
            vmem((1024, 512), BF16), vmem((1024, 512), BF16), vmem((512, 1024), BF16), vmem((512, 1024), BF16),
            vmem((256, 1024), BF16), vmem((256, 1024), BF16), vmem((512, 1024), BF16), vmem((512, 1024), BF16),
            vmem((512, 512), F32), vmem((256, 512), BF16), vmem((256, 512), BF16),
            vmem((2, 128, 512), BF16), vmem((2, 128, 512), BF16), vmem((1024, 128), F32),
            vmem((1024, 256), F32), vmem((512, 256), F32), vmem((4, 2, 128, 256), F32), vmem((7, 64, 256), F32),
            vmem((64, 512), F32), vmem((128, 128), F32), vmem((16, 8, 128), F32),
            vmem((2, 128, 512), F32), vmem((2, 256, 128), F32), vmem((2, 16, 16, 128), F32), vmem((16, 1024), F32),
            vmem((16, 512), F32), vmem((7, 16, 512), F32),
            dma((4,)), dma((4,)), dma((4,)), dma((4, 4)), dma((4, 4)), dma, dma, dma((4,)), dma((2, 2)),
            dma((2, 4)), dma((2, 4)), dma, dma,
            dma((4, 2)), dma((4, 2)), dma((7,)), dma((7,)), dma((3,)), dma((3,)), dma((16,)), dma((16,)),
            dma((2, 16)), dma((2, 16)), dma((7,)), dma((7,)),
        ],
        compiler_params=pltpu.CompilerParams(
            collective_id=0, has_side_effects=True, vmem_limit_bytes=40 * 1024 * 1024
        ),
        name="cholesky_step",
    )(*(pltpu.with_memory_space_constraint(a, pltpu.HBM) for a in operands))
    return (grad.T, diag)


def solution(mesh):
    in_specs = (P("row", "col"), P("row", "col"), P("row", "col"), P())
    out_specs = (P("row", "col"), P("col", None))
    return jax.shard_map(body, mesh=mesh, in_specs=in_specs, out_specs=out_specs, check_vma=False)
```

```python
import functools

import jax
import jax.numpy as jnp
from jax import lax
from jax.experimental import pallas as pl
from jax.experimental.pallas import tpu as pltpu
from jax.sharding import PartitionSpec as P

F32 = jnp.float32
BF16 = jnp.bfloat16
MESH = pl.DeviceIdType.MESH
NT = (((1,), (1,)), ((), ()))


def split(value):
    high = value.astype(BF16)
    low = (value - high.astype(F32)).astype(BF16)
    return high, low


def dot3(a_high, a_low, b_high, b_low):
    def one(a, b):
        return lax.dot_general(a, b, NT, preferred_element_type=F32)

    return one(a_high, b_low) + one(a_low, b_high) + one(a_high, b_high)


def aligned(start, size):
    return pl.ds(pl.multiple_of(start, size), size)


def kernel(
    a_hbm, panel_hbm, pa_hbm, inv_hbm, grad_ref, diag_ref,
    panel_v, pa_v, inv_v, wide, s_raw, pf, pc, s_hi, s_lo, st_hi, st_lo,
    p_hi, p_lo, f_hi, f_lo, inv_r, it_hi, it_lo, iq_hi, iq_lo, pa_r, out1, out2, ry, rr,
    qadj, gq, rgq, adj, gt, rg, gfull, dpart, rd,
    local_sem, agz_s, agz_r, agy_s, agy_r, sa_s, sa_r, mini_s, mini_r, pc_s, pc_r, po_s, po_r,
    ry_s, ry_r, rr_s, rr_r, f_s, f_r, rgq_s, rgq_r, rg_s, rg_r, rd_s, rd_r,
):
    r = lax.axis_index("row")
    c = lax.axis_index("col")
    zl, x = r // 4, r % 4
    y, z, p = c // 8, (c // 2) % 4, c % 2
    yz = y * 4 + z

    def dev(zl_, x_, y_, z_, p_):
        return (zl_ * 4 + x_, (y_ * 4 + z_) * 2 + p_)

    def remote(src, dst, send, recv, target):
        return pltpu.make_async_remote_copy(
            src_ref=src, dst_ref=dst, send_sem=send, recv_sem=recv,
            device_id=target, device_id_type=MESH,
        )

    sibling = dev(zl, x, y, z, 1 - p)

    def arrived(ref, send, recv):
        remote(ref, ref, send, recv, sibling).wait_recv()

    barrier = pltpu.get_barrier_semaphore()
    greet = [sibling]
    greet += [dev(zl, x, y, (z + j) % 4, p) for j in (1, 2, 3)]
    greet += [dev(zl, x, (y + j) % 4, z, p) for j in (1, 2, 3)]
    row_offsets = [(a, b) for a in (0, 1) for b in (0, 1, 2, 3) if (a, b) != (0, 0)]
    greet += [dev((zl + a) % 2, (x + b) % 4, y, z, p) for a, b in row_offsets]
    for target in greet:
        pl.semaphore_signal(barrier, inc=1, device_id=target, device_id_type=MESH)
    to_row, to_z = (z // 2) * 4 + y, r // 2
    keeps = jnp.logical_and(to_row == r, to_z == z)
    for b in (0, 1):
        for h in (0, 1):
            is_me = jnp.logical_and(keeps, jnp.logical_and(r % 2 == b, z % 2 == h))

            @pl.when(jnp.logical_not(is_me))
            def _():
                pl.semaphore_signal(
                    barrier, inc=1, device_id=(2 * z + b, (x * 4 + zl * 2 + h) * 2 + p),
                    device_id_type=MESH,
                )

    load_panel = pltpu.make_async_copy(panel_hbm, panel_v, local_sem.at[0])
    load_a = pltpu.make_async_copy(a_hbm, s_raw.at[p], local_sem.at[1])
    load_pa = pltpu.make_async_copy(pa_hbm, pa_v, local_sem.at[2])
    load_inv = pltpu.make_async_copy(inv_hbm, inv_v, local_sem.at[3])
    load_panel.start()
    load_a.start()
    load_pa.start()
    load_inv.start()

    left = lax.broadcasted_iota(jnp.int32, (16, 128), 1) < 64

    def ordered(ref, t):
        w1 = t // 2 + 8 * (t % 2)
        one = ref[:, 128 * (w1 // 2):128 * (w1 // 2) + 128]
        two = ref[:, 128 * (w1 // 2 + 2):128 * (w1 // 2 + 2) + 128]
        if w1 % 2:
            one = pltpu.roll(one, 64, 1)
        else:
            two = pltpu.roll(two, 64, 1)
        return jnp.where(left, one, two)

    load_panel.wait()
    for t in range(8):
        pf[yz, p, :, 128 * t:128 * t + 128] = ordered(panel_v, t)

    pl.semaphore_wait(barrier, len(greet) + 3 + jnp.where(keeps, 0, 1))

    sends = []
    conditional = []

    def drain():
        while sends:
            sends.pop().wait_send()
        while conditional:
            cond, cp = conditional.pop()
            pl.when(cond)(cp.wait_send)


    for j in (2, 1, 3, 0):
        y2 = (y + j) % 4
        src = pf.at[yz, p, :, aligned(256 * y2, 256)]
        dst = pc.at[aligned(16 * yz, 16), aligned(256 * (r % 2), 256)]
        cp = remote(src, dst, mini_s.at[j], mini_r.at[r % 2, z % 2], (to_row, (y2 * 4 + to_z) * 2 + p))
        if j:
            cp.start()
            sends.append(cp)
        else:
            pl.when(jnp.logical_not(keeps))(cp.start)
            conditional.append((jnp.logical_not(keeps), cp))

    @pl.when(keeps)
    def _():
        pc[aligned(16 * yz, 16), aligned(256 * (r % 2), 256)] = pf[yz, p, :, aligned(256 * y, 256)]

    for j in (1, 3, 2):
        cp = remote(pf.at[yz, p], pf.at[yz, p], agz_s.at[j], agz_r.at[j], dev(zl, x, y, (z + j) % 4, p))
        cp.start()
        sends.append(cp)

    def forward_y(k):
        slot = y * 4 + (z + 4 - k) % 4
        for j in (1, 3, 2):
            cp = remote(
                pf.at[slot, p], pf.at[slot, p], agy_s.at[j, k], agy_r.at[j, k],
                dev(zl, x, (y + j) % 4, z, p),
            )
            cp.start()
            sends.append(cp)

    forward_y(0)
    load_a.wait()
    cp_a = remote(s_raw.at[p], s_raw.at[p], sa_s, sa_r, sibling)
    cp_a.start()
    sends.append(cp_a)

    lane = lax.broadcasted_iota(jnp.int32, (128, 256), 1)
    line = lax.broadcasted_iota(jnp.int32, (128, 256), 0)

    def col_nat(b):
        return (32 * (lane // 64) + c - p + b) * 64 + lane % 64

    def prepare(b):
        cols = (32 * (lane // 64) + c - p + b) * 64 + lane % 64

        def step(t, carry):
            w1 = t // 2 + 8 * (t % 2)
            rows = jnp.concatenate(
                [s_raw[b, aligned(64 * w1, 64), :], s_raw[b, aligned(64 * w1 + 256, 64), :]], axis=0
            )
            row_nat = (8 * w1 + r) * 64 + line + jnp.where(line >= 64, 32 * 64 - 64, 0)
            value = jnp.where(row_nat >= cols, rows, 0.0)
            high, low = split(value)
            s_hi[aligned(128 * t, 128), aligned(256 * b, 256)] = high
            s_lo[aligned(128 * t, 128), aligned(256 * b, 256)] = low
            high, low = split(value.T)
            st_hi[aligned(256 * b, 256), aligned(128 * t, 128)] = high
            st_lo[aligned(256 * b, 256), aligned(128 * t, 128)] = low
            return carry

        lax.fori_loop(0, 8, step, 0)

    for k in (1, 3, 2):
        arrived(pf.at[0, 0], agz_s.at[k], agz_r.at[k])
        forward_y(k)

    for b in (0, 1):
        for h in (0, 1):
            is_me = jnp.logical_and(keeps, jnp.logical_and(r % 2 == b, z % 2 == h))

            @pl.when(jnp.logical_not(is_me))
            def _():
                arrived(pc.at[0:16, 0:256], mini_s.at[0], mini_r.at[b, h])

    part = pc.at[aligned(32 * (2 * x + zl), 32)]
    for a, b in ((1, 2), (1, 1), (1, 3), (1, 0), (0, 2), (0, 1), (0, 3)):
        cp = remote(part, part, pc_s.at[a, b], pc_r.at[a, b], dev((zl + a) % 2, (x + b) % 4, y, z, p))
        cp.start()
        sends.append(cp)
    prepare(p)
    load_pa.wait()
    wide[...] = jnp.zeros_like(wide)
    for t in range(8):
        wide[aligned(16 * (yz % 8), 16), 128 * t:128 * t + 128] = ordered(pa_v, t)
    for t in range(8):
        pa_r[128 * t:128 * t + 128, :] = wide[:, 128 * t:128 * t + 128].T

    arrived(s_raw.at[0], sa_s, sa_r)
    prepare(1 - p)
    for a, b in row_offsets:
        arrived(pc.at[0:32], pc_s.at[a, b], pc_r.at[a, b])

    pc_hi, pc_lo = split(pc[...])
    tile = aligned(128 * (y // 2), 128)
    for h, j in ((0, 1), (0, 3), (0, 2), (1, 1), (1, 3), (1, 2)):
        rows = aligned(256 * ((y + j) % 4) + 128 * h, 128)
        out1[rows, :] = dot3(s_hi[rows, :], s_lo[rows, :], pc_hi, pc_lo)
        out1[rows, tile] = out1[rows, tile] - pa_r[rows, :]
        cp = remote(
            out1.at[rows], ry.at[j, h], ry_s.at[j, h], ry_r.at[j, h], dev(zl, x, (y + j) % 4, z, p)
        )
        cp.start()
        sends.append(cp)

    for j in (1, 3, 2):
        for k in range(4):
            arrived(pf.at[0, 0], agy_s.at[j, k], agy_r.at[j, k])
    cp = remote(pf.at[:, p], pf.at[:, p], po_s, po_r, sibling)
    cp.start()
    sends.append(cp)
    for k in range(16):
        high, low = split(pf[k, p])
        p_hi[16 * k:16 * k + 16, :] = high
        p_lo[16 * k:16 * k + 16, :] = low
    for b in (0, 1):
        rows = pl.ds(256 * b, 256)
        out2[rows, :] = dot3(st_hi[rows, :], st_lo[rows, :], p_hi[...], p_lo[...])
    for i, (a, b) in enumerate(row_offsets):
        piece = ((zl + a) % 2) * 4 + (x + b) % 4
        cp = remote(
            out2.at[aligned(64 * piece, 64)], rr.at[i], rr_s.at[i], rr_r.at[i],
            dev((zl + a) % 2, (x + b) % 4, y, z, p),
        )
        cp.start()
        sends.append(cp)

    for h in (0, 1):
        rows = aligned(256 * y + 128 * h, 128)
        out1[rows, :] = dot3(s_hi[rows, :], s_lo[rows, :], pc_hi, pc_lo)
        out1[rows, tile] = out1[rows, tile] - pa_r[rows, :]

    load_inv.wait()
    for k in range(16):
        for b in (0, 1):
            inv_r[256 * b + 16 * k:256 * b + 16 * k + 16, :] = -inv_v[(2 * k + b) * 16:(2 * k + b) * 16 + 16, :]
    for t in range(4):
        inv_v[128 * t:128 * t + 128, :] = inv_r[:, 128 * t:128 * t + 128].T
    for k in range(16):
        high, low = split(inv_v[aligned((2 * k + p) * 16, 16), :])
        it_hi[16 * k:16 * k + 16, :] = high
        it_lo[16 * k:16 * k + 16, :] = low

    for k in range(8):
        for e in (0, 1):
            first = inv_v[aligned((4 * k + p) * 16 + 8 * e, 8), :]
            second = inv_v[aligned((4 * k + 2 + p) * 16 + 8 * e, 8), :]
            high, low = split(jnp.concatenate([first, second], axis=0))
            iq_hi[e, 16 * k:16 * k + 16, :] = high
            iq_lo[e, 16 * k:16 * k + 16, :] = low

    own = aligned(256 * p, 256)
    offsets = [(dy, dz) for dz in (2, 1, 3, 0) for dy in (2, 1, 3, 0)]
    others = offsets[:-1]

    def swap(ref, k):
        cp = remote(ref, ref, f_s.at[k], f_r.at[k], sibling)
        cp.start()
        sends.append(cp)

    def sum_y(h):
        for j in (1, 3, 2):
            arrived(ry.at[0, 0], ry_s.at[j, h], ry_r.at[j, h])
        adj[h, :, own] = (
            out1[aligned(256 * y + 128 * h, 128), :] + ry[1, h] + ry[2, h] + ry[3, h]
        )
        swap(adj.at[h, :, own], h)

    def to_owners(h):
        arrived(adj.at[h, :, 0:256], f_s.at[h], f_r.at[h])
        a_hi, a_lo = split(adj[h])
        gt[h] = dot3(it_hi[...], it_lo[...], a_hi, a_lo)
        for dy, dz in others:
            i = dy * 4 + dz
            y2, z2 = (y + dy) % 4, (z + dz) % 4
            cp = remote(
                gt.at[h, aligned(16 * (y2 * 4 + z2), 16)], rg.at[h, yz], rg_s.at[h, i], rg_r.at[h, i],
                dev(zl, x, y2, z2, p),
            )
            cp.start()
            sends.append(cp)
        rg[h, yz] = gt[h, aligned(16 * yz, 16), :]

    sum_y(0)
    to_owners(0)

    total = out2[aligned(64 * r, 64), :]
    for i in range(7):
        arrived(rr.at[i], rr_s.at[i], rr_r.at[i])
        total = total + rr[i]
    qadj[:, own] = total
    swap(qadj.at[:, own], 2)
    sum_y(1)

    arrived(qadj.at[:, 0:256], f_s.at[2], f_r.at[2])
    a_hi, a_lo = split(qadj[...])
    none = jnp.zeros((64, 512), BF16)
    gq[...] = dot3(
        iq_hi[0], iq_lo[0], jnp.concatenate([a_hi, none], axis=0), jnp.concatenate([a_lo, none], axis=0)
    ) + dot3(
        iq_hi[1], iq_lo[1], jnp.concatenate([none, a_hi], axis=0), jnp.concatenate([none, a_lo], axis=0)
    )
    q_row, q_slot = 2 * z + zl, y * 4 + x
    stays = q_row == r
    moves = jnp.logical_not(stays)
    for dy, dz in offsets:
        i = dy * 4 + dz
        to = ((y + dy) % 4) * 4 + (z + dz) % 4
        cp = remote(
            gq.at[aligned(8 * to, 8)], rgq.at[q_slot], rgq_s.at[i], rgq_r.at[q_slot], (q_row, to * 2 + p)
        )
        if i:
            cp.start()
            sends.append(cp)
        else:
            pl.when(moves)(cp.start)
            conditional.append((moves, cp))

    @pl.when(stays)
    def _():
        rgq[q_slot] = gq[aligned(8 * yz, 8), :]

    to_owners(1)

    arrived(pf.at[:, 0], po_s, po_r)
    for k in range(16):
        for b in (0, 1):
            high, low = split(pf[k, b])
            f_hi[32 * k + 16 * b:32 * k + 16 * b + 16, :] = high
            f_lo[32 * k + 16 * b:32 * k + 16 * b + 16, :] = low

    drain()
    for h in (0, 1):
        for dy, dz in others:
            i = dy * 4 + dz
            arrived(rg.at[0, 0], rg_s.at[h, i], rg_r.at[h, i])
    for slot in range(16):
        @pl.when(jnp.logical_not(jnp.logical_and(stays, q_slot == slot)))
        def _():
            arrived(rgq.at[0], rgq_s.at[0], rgq_r.at[slot])

    low_half = left[0:8]
    for t in range(8):
        h, g = t % 2, 4 * (t // 2)
        parts = (rg[h, g] + rg[h, g + 1]) + (rg[h, g + 2] + rg[h, g + 3])
        one, two = rgq[2 * t], rgq[2 * t + 1]
        upper = jnp.where(low_half, one, pltpu.roll(two, 64, 1))
        lower = jnp.where(low_half, pltpu.roll(one, 64, 1), two)
        gfull[:, 128 * t:128 * t + 128] = parts + jnp.concatenate([upper, lower], axis=0)

    g_hi, g_lo = split(gfull[...])
    both = lax.dot_general(
        jnp.concatenate([g_hi, g_lo], axis=0), f_hi[...], NT, preferred_element_type=F32
    )
    cross = lax.dot_general(g_hi, f_lo[...], NT, preferred_element_type=F32)
    dpart[...] = both[0:16, :] + (both[16:32, :] + cross)
    for a, b in ((1, 2), (0, 2), (1, 1), (1, 3), (1, 0), (0, 1), (0, 3)):
        i = a * 4 + b - 1
        cp = remote(
            dpart, rd.at[i], rd_s.at[i], rd_r.at[i], dev((zl + a) % 2, (x + b) % 4, y, z, p)
        )
        cp.start()
        sends.append(cp)
    for t in range(8):
        w = 2 * t
        k1 = (w % 4) * 4 + w // 4
        k2 = k1 + 4
        one = gfull[:, 128 * (k1 // 2):128 * (k1 // 2) + 128]
        two = gfull[:, 128 * (k2 // 2):128 * (k2 // 2) + 128]
        if k1 % 2:
            one = pltpu.roll(one, 64, 1)
        else:
            two = pltpu.roll(two, 64, 1)
        grad_ref[:, 128 * t:128 * t + 128] = jnp.where(left, one, two)
    for i in range(7):
        arrived(rd.at[i], rd_s.at[i], rd_r.at[i])
    total = jnp.zeros((16, 512), F32)
    for q in range(8):
        a, b = (zl + 2 - q // 4) % 2, (x + 4 - q % 4) % 4
        slot = a * 4 + b
        keep = jnp.where(slot == 0, dpart[...], rd[jnp.maximum(slot - 1, 0)])
        total = total + keep
    diag_row = c * 16 + lax.broadcasted_iota(jnp.int32, (16, 512), 0)
    diag_col = lax.broadcasted_iota(jnp.int32, (16, 512), 1)
    diag_ref[...] = jnp.where(diag_row >= diag_col, -total, 0.0)

    drain()


def body(adj_trailing, panel, panel_adjoint, inverse_diag):
    vmem, dma = pltpu.VMEM, pltpu.SemaphoreType.DMA
    operands = (adj_trailing, panel.T, panel_adjoint.T, inverse_diag)
    grad, diag = pl.pallas_call(
        kernel,
        out_shape=(
            jax.ShapeDtypeStruct((16, 1024), F32),
            jax.ShapeDtypeStruct((16, 512), F32),
        ),
        in_specs=[pl.BlockSpec(memory_space=pl.ANY)] * 4,
        out_specs=(pl.BlockSpec(memory_space=vmem), pl.BlockSpec(memory_space=vmem)),
        scratch_shapes=[
            vmem((16, 1024), F32), vmem((16, 1024), F32), vmem((512, 512), F32), vmem((128, 1024), F32),
            vmem((2, 1024, 256), F32), vmem((16, 2, 16, 1024), F32), vmem((256, 512), F32),
            vmem((1024, 512), BF16), vmem((1024, 512), BF16), vmem((512, 1024), BF16), vmem((512, 1024), BF16),
            vmem((256, 1024), BF16), vmem((256, 1024), BF16), vmem((512, 1024), BF16), vmem((512, 1024), BF16),
            vmem((512, 512), F32), vmem((256, 512), BF16), vmem((256, 512), BF16),
            vmem((2, 128, 512), BF16), vmem((2, 128, 512), BF16), vmem((1024, 128), F32),
            vmem((1024, 256), F32), vmem((512, 256), F32), vmem((4, 2, 128, 256), F32), vmem((7, 64, 256), F32),
            vmem((64, 512), F32), vmem((128, 128), F32), vmem((16, 8, 128), F32),
            vmem((2, 128, 512), F32), vmem((2, 256, 128), F32), vmem((2, 16, 16, 128), F32), vmem((16, 1024), F32),
            vmem((16, 512), F32), vmem((7, 16, 512), F32),
            dma((4,)), dma((4,)), dma((4,)), dma((4, 4)), dma((4, 4)), dma, dma, dma((4,)), dma((2, 2)),
            dma((2, 4)), dma((2, 4)), dma, dma,
            dma((4, 2)), dma((4, 2)), dma((7,)), dma((7,)), dma((3,)), dma((3,)), dma((16,)), dma((16,)),
            dma((2, 16)), dma((2, 16)), dma((7,)), dma((7,)),
        ],
        compiler_params=pltpu.CompilerParams(
            collective_id=0, has_side_effects=True, vmem_limit_bytes=40 * 1024 * 1024
        ),
        name="cholesky_step",
    )(*(pltpu.with_memory_space_constraint(a, pltpu.HBM) for a in operands))
    return (grad.T, diag)


def solution(mesh):
    in_specs = (P("row", "col"), P("row", "col"), P("row", "col"), P())
    out_specs = (P("row", "col"), P("col", None))
    return jax.shard_map(body, mesh=mesh, in_specs=in_specs, out_specs=out_specs, check_vma=False)
```

```python
import functools

import jax
import jax.numpy as jnp
from jax import lax
from jax.experimental import pallas as pl
from jax.experimental.pallas import tpu as pltpu
from jax.sharding import PartitionSpec as P

F32 = jnp.float32
BF16 = jnp.bfloat16
MESH = pl.DeviceIdType.MESH
NT = (((1,), (1,)), ((), ()))


def split(value):
    high = value.astype(BF16)
    low = (value - high.astype(F32)).astype(BF16)
    return high, low


def dot3(a_high, a_low, b_high, b_low):
    def one(a, b):
        return lax.dot_general(a, b, NT, preferred_element_type=F32)

    return one(a_high, b_low) + one(a_low, b_high) + one(a_high, b_high)


def aligned(start, size):
    return pl.ds(pl.multiple_of(start, size), size)


def kernel(
    a_hbm, panel_hbm, pa_hbm, inv_hbm, grad_ref, diag_ref,
    panel_v, pa_v, inv_v, wide, s_raw, pf, pc, s_hi, s_lo, st_hi, st_lo,
    p_hi, p_lo, f_hi, f_lo, inv_r, it_hi, it_lo, iq_hi, iq_lo, pa_r, out1, out2, ry, rr,
    qadj, gq, rgq, adj, gt, rg, gfull, dpart, rd,
    local_sem, agz_s, agz_r, agy_s, agy_r, sa_s, sa_r, mini_s, mini_r, pc_s, pc_r, po_s, po_r,
    ry_s, ry_r, rr_s, rr_r, f_s, f_r, rgq_s, rgq_r, rg_s, rg_r, rd_s, rd_r,
):
    r = lax.axis_index("row")
    c = lax.axis_index("col")
    zl, x = r // 4, r % 4
    y, z, p = c // 8, (c // 2) % 4, c % 2
    yz = y * 4 + z

    def dev(zl_, x_, y_, z_, p_):
        return (zl_ * 4 + x_, (y_ * 4 + z_) * 2 + p_)

    def remote(src, dst, send, recv, target):
        return pltpu.make_async_remote_copy(
            src_ref=src, dst_ref=dst, send_sem=send, recv_sem=recv,
            device_id=target, device_id_type=MESH,
        )

    sibling = dev(zl, x, y, z, 1 - p)

    def arrived(ref, send, recv):
        remote(ref, ref, send, recv, sibling).wait_recv()

    barrier = pltpu.get_barrier_semaphore()
    greet = [sibling]
    greet += [dev(zl, x, y, (z + j) % 4, p) for j in (1, 2, 3)]
    greet += [dev(zl, x, (y + j) % 4, z, p) for j in (1, 2, 3)]
    row_offsets = [(a, b) for a in (0, 1) for b in (0, 1, 2, 3) if (a, b) != (0, 0)]
    greet += [dev((zl + a) % 2, (x + b) % 4, y, z, p) for a, b in row_offsets]
    for target in greet:
        pl.semaphore_signal(barrier, inc=1, device_id=target, device_id_type=MESH)
    to_row, to_z = (z // 2) * 4 + y, r // 2
    keeps = jnp.logical_and(to_row == r, to_z == z)
    for b in (0, 1):
        for h in (0, 1):
            is_me = jnp.logical_and(keeps, jnp.logical_and(r % 2 == b, z % 2 == h))

            @pl.when(jnp.logical_not(is_me))
            def _():
                pl.semaphore_signal(
                    barrier, inc=1, device_id=(2 * z + b, (x * 4 + zl * 2 + h) * 2 + p),
                    device_id_type=MESH,
                )

    load_panel = pltpu.make_async_copy(panel_hbm, panel_v, local_sem.at[0])
    load_a = pltpu.make_async_copy(a_hbm, s_raw.at[p], local_sem.at[1])
    load_pa = pltpu.make_async_copy(pa_hbm, pa_v, local_sem.at[2])
    load_inv = pltpu.make_async_copy(inv_hbm, inv_v, local_sem.at[3])
    load_panel.start()
    load_a.start()
    load_pa.start()
    load_inv.start()

    left = lax.broadcasted_iota(jnp.int32, (16, 128), 1) < 64

    def ordered(ref, t):
        w1 = t // 2 + 8 * (t % 2)
        one = ref[:, 128 * (w1 // 2):128 * (w1 // 2) + 128]
        two = ref[:, 128 * (w1 // 2 + 2):128 * (w1 // 2 + 2) + 128]
        if w1 % 2:
            one = pltpu.roll(one, 64, 1)
        else:
            two = pltpu.roll(two, 64, 1)
        return jnp.where(left, one, two)

    load_panel.wait()
    for t in range(8):
        pf[yz, p, :, 128 * t:128 * t + 128] = ordered(panel_v, t)

    pl.semaphore_wait(barrier, len(greet) + 3 + jnp.where(keeps, 0, 1))

    sends = []
    conditional = []

    def drain():
        while sends:
            sends.pop().wait_send()
        while conditional:
            cond, cp = conditional.pop()
            pl.when(cond)(cp.wait_send)


    for j in (2, 1, 3, 0):
        y2 = (y + j) % 4
        src = pf.at[yz, p, :, aligned(256 * y2, 256)]
        dst = pc.at[aligned(16 * yz, 16), aligned(256 * (r % 2), 256)]
        cp = remote(src, dst, mini_s.at[j], mini_r.at[r % 2, z % 2], (to_row, (y2 * 4 + to_z) * 2 + p))
        if j:
            cp.start()
            sends.append(cp)
        else:
            pl.when(jnp.logical_not(keeps))(cp.start)
            conditional.append((jnp.logical_not(keeps), cp))

    @pl.when(keeps)
    def _():
        pc[aligned(16 * yz, 16), aligned(256 * (r % 2), 256)] = pf[yz, p, :, aligned(256 * y, 256)]

    for j in (1, 3, 2):
        cp = remote(pf.at[yz, p], pf.at[yz, p], agz_s.at[j], agz_r.at[j], dev(zl, x, y, (z + j) % 4, p))
        cp.start()
        sends.append(cp)

    def forward_y(k):
        slot = y * 4 + (z + 4 - k) % 4
        for j in (1, 3, 2):
            cp = remote(
                pf.at[slot, p], pf.at[slot, p], agy_s.at[j, k], agy_r.at[j, k],
                dev(zl, x, (y + j) % 4, z, p),
            )
            cp.start()
            sends.append(cp)

    forward_y(0)
    load_a.wait()
    cp_a = remote(s_raw.at[p], s_raw.at[p], sa_s, sa_r, sibling)
    cp_a.start()
    sends.append(cp_a)

    lane = lax.broadcasted_iota(jnp.int32, (128, 256), 1)
    line = lax.broadcasted_iota(jnp.int32, (128, 256), 0)

    def col_nat(b):
        return (32 * (lane // 64) + c - p + b) * 64 + lane % 64

    def prepare(b):
        cols = (32 * (lane // 64) + c - p + b) * 64 + lane % 64

        def step(t, carry):
            w1 = t // 2 + 8 * (t % 2)
            rows = jnp.concatenate(
                [s_raw[b, aligned(64 * w1, 64), :], s_raw[b, aligned(64 * w1 + 256, 64), :]], axis=0
            )
            row_nat = (8 * w1 + r) * 64 + line + jnp.where(line >= 64, 32 * 64 - 64, 0)
            value = jnp.where(row_nat >= cols, rows, 0.0)
            high, low = split(value)
            s_hi[aligned(128 * t, 128), aligned(256 * b, 256)] = high
            s_lo[aligned(128 * t, 128), aligned(256 * b, 256)] = low
            high, low = split(value.T)
            st_hi[aligned(256 * b, 256), aligned(128 * t, 128)] = high
            st_lo[aligned(256 * b, 256), aligned(128 * t, 128)] = low
            return carry

        lax.fori_loop(0, 8, step, 0)

    for k in (1, 3, 2):
        arrived(pf.at[0, 0], agz_s.at[k], agz_r.at[k])
        forward_y(k)

    for b in (0, 1):
        for h in (0, 1):
            is_me = jnp.logical_and(keeps, jnp.logical_and(r % 2 == b, z % 2 == h))

            @pl.when(jnp.logical_not(is_me))
            def _():
                arrived(pc.at[0:16, 0:256], mini_s.at[0], mini_r.at[b, h])

    part = pc.at[aligned(32 * (2 * x + zl), 32)]
    for a, b in ((1, 2), (1, 1), (1, 3), (1, 0), (0, 2), (0, 1), (0, 3)):
        cp = remote(part, part, pc_s.at[a, b], pc_r.at[a, b], dev((zl + a) % 2, (x + b) % 4, y, z, p))
        cp.start()
        sends.append(cp)
    prepare(p)
    load_pa.wait()
    wide[...] = jnp.zeros_like(wide)
    for t in range(8):
        wide[aligned(16 * (yz % 8), 16), 128 * t:128 * t + 128] = ordered(pa_v, t)
    for t in range(8):
        pa_r[128 * t:128 * t + 128, :] = wide[:, 128 * t:128 * t + 128].T

    arrived(s_raw.at[0], sa_s, sa_r)
    prepare(1 - p)
    for a, b in row_offsets:
        arrived(pc.at[0:32], pc_s.at[a, b], pc_r.at[a, b])

    pc_hi, pc_lo = split(pc[...])
    tile = aligned(128 * (y // 2), 128)
    for h, j in ((0, 1), (0, 3), (0, 2), (1, 1), (1, 3), (1, 2)):
        rows = aligned(256 * ((y + j) % 4) + 128 * h, 128)
        out1[rows, :] = dot3(s_hi[rows, :], s_lo[rows, :], pc_hi, pc_lo)
        out1[rows, tile] = out1[rows, tile] - pa_r[rows, :]
        cp = remote(
            out1.at[rows], ry.at[j, h], ry_s.at[j, h], ry_r.at[j, h], dev(zl, x, (y + j) % 4, z, p)
        )
        cp.start()
        sends.append(cp)

    for j in (1, 3, 2):
        for k in range(4):
            arrived(pf.at[0, 0], agy_s.at[j, k], agy_r.at[j, k])
    cp = remote(pf.at[:, p], pf.at[:, p], po_s, po_r, sibling)
    cp.start()
    sends.append(cp)
    for k in range(16):
        high, low = split(pf[k, p])
        p_hi[16 * k:16 * k + 16, :] = high
        p_lo[16 * k:16 * k + 16, :] = low
    for b in (0, 1):
        rows = pl.ds(256 * b, 256)
        out2[rows, :] = dot3(st_hi[rows, :], st_lo[rows, :], p_hi[...], p_lo[...])
    for i, (a, b) in enumerate(row_offsets):
        piece = ((zl + a) % 2) * 4 + (x + b) % 4
        cp = remote(
            out2.at[aligned(64 * piece, 64)], rr.at[i], rr_s.at[i], rr_r.at[i],
            dev((zl + a) % 2, (x + b) % 4, y, z, p),
        )
        cp.start()
        sends.append(cp)

    for h in (0, 1):
        rows = aligned(256 * y + 128 * h, 128)
        out1[rows, :] = dot3(s_hi[rows, :], s_lo[rows, :], pc_hi, pc_lo)
        out1[rows, tile] = out1[rows, tile] - pa_r[rows, :]

    load_inv.wait()
    for k in range(16):
        for b in (0, 1):
            inv_r[256 * b + 16 * k:256 * b + 16 * k + 16, :] = -inv_v[(2 * k + b) * 16:(2 * k + b) * 16 + 16, :]
    for t in range(4):
        inv_v[128 * t:128 * t + 128, :] = inv_r[:, 128 * t:128 * t + 128].T
    for k in range(16):
        high, low = split(inv_v[aligned((2 * k + p) * 16, 16), :])
        it_hi[16 * k:16 * k + 16, :] = high
        it_lo[16 * k:16 * k + 16, :] = low

    for k in range(8):
        for e in (0, 1):
            first = inv_v[aligned((4 * k + p) * 16 + 8 * e, 8), :]
            second = inv_v[aligned((4 * k + 2 + p) * 16 + 8 * e, 8), :]
            high, low = split(jnp.concatenate([first, second], axis=0))
            iq_hi[128 * e + 16 * k:128 * e + 16 * k + 16, :] = high
            iq_lo[128 * e + 16 * k:128 * e + 16 * k + 16, :] = low

    own = aligned(256 * p, 256)
    offsets = [(dy, dz) for dz in (2, 1, 3, 0) for dy in (2, 1, 3, 0)]
    others = offsets[:-1]

    def swap(ref, k):
        cp = remote(ref, ref, f_s.at[k], f_r.at[k], sibling)
        cp.start()
        sends.append(cp)

    def sum_y(h):
        for j in (1, 3, 2):
            arrived(ry.at[0, 0], ry_s.at[j, h], ry_r.at[j, h])
        adj[h, :, own] = (
            out1[aligned(256 * y + 128 * h, 128), :] + ry[1, h] + ry[2, h] + ry[3, h]
        )
        swap(adj.at[h, :, own], h)

    def to_owners(h):
        arrived(adj.at[h, :, 0:256], f_s.at[h], f_r.at[h])
        a_hi, a_lo = split(adj[h])
        gt[h] = dot3(it_hi[...], it_lo[...], a_hi, a_lo)
        for dy, dz in others:
            i = dy * 4 + dz
            y2, z2 = (y + dy) % 4, (z + dz) % 4
            cp = remote(
                gt.at[h, aligned(16 * (y2 * 4 + z2), 16)], rg.at[h, yz], rg_s.at[h, i], rg_r.at[h, i],
                dev(zl, x, y2, z2, p),
            )
            cp.start()
            sends.append(cp)
        rg[h, yz] = gt[h, aligned(16 * yz, 16), :]

    sum_y(0)
    to_owners(0)

    total = out2[aligned(64 * r, 64), :]
    for i in range(7):
        arrived(rr.at[i], rr_s.at[i], rr_r.at[i])
        total = total + rr[i]
    qadj[:, own] = total
    swap(qadj.at[:, own], 2)
    sum_y(1)

    arrived(qadj.at[:, 0:256], f_s.at[2], f_r.at[2])
    a_hi, a_lo = split(qadj[...])
    both = dot3(iq_hi[...], iq_lo[...], a_hi, a_lo)
    gq[...] = jnp.concatenate([both[0:128, :], both[128:256, :]], axis=1)
    q_row, q_slot = 2 * z + zl, y * 4 + x
    stays = q_row == r
    moves = jnp.logical_not(stays)
    for dy, dz in offsets:
        i = dy * 4 + dz
        to = ((y + dy) % 4) * 4 + (z + dz) % 4
        cp = remote(
            gq.at[aligned(8 * to, 8)], rgq.at[q_slot], rgq_s.at[i], rgq_r.at[q_slot], (q_row, to * 2 + p)
        )
        if i:
            cp.start()
            sends.append(cp)
        else:
            pl.when(moves)(cp.start)
            conditional.append((moves, cp))

    @pl.when(stays)
    def _():
        rgq[q_slot] = gq[aligned(8 * yz, 8), :]

    to_owners(1)

    arrived(pf.at[:, 0], po_s, po_r)
    for k in range(16):
        for b in (0, 1):
            high, low = split(pf[k, b])
            f_hi[32 * k + 16 * b:32 * k + 16 * b + 16, :] = high
            f_lo[32 * k + 16 * b:32 * k + 16 * b + 16, :] = low

    drain()
    for h in (0, 1):
        for dy, dz in others:
            i = dy * 4 + dz
            arrived(rg.at[0, 0], rg_s.at[h, i], rg_r.at[h, i])
    for slot in range(16):
        @pl.when(jnp.logical_not(jnp.logical_and(stays, q_slot == slot)))
        def _():
            arrived(rgq.at[0], rgq_s.at[0], rgq_r.at[slot])

    low_half = left[0:8]
    for t in range(8):
        h, g = t % 2, 4 * (t // 2)
        parts = (rg[h, g] + rg[h, g + 1]) + (rg[h, g + 2] + rg[h, g + 3])
        one, two = rgq[2 * t], rgq[2 * t + 1]
        upper = jnp.where(low_half, one, pltpu.roll(two, 64, 1))
        lower = jnp.where(low_half, pltpu.roll(one, 64, 1), two)
        gfull[:, 128 * t:128 * t + 128] = parts + jnp.concatenate([upper, lower], axis=0)

    g_hi, g_lo = split(gfull[...])
    both = lax.dot_general(
        jnp.concatenate([g_hi, g_lo], axis=0), f_hi[...], NT, preferred_element_type=F32
    )
    cross = lax.dot_general(g_hi, f_lo[...], NT, preferred_element_type=F32)
    dpart[...] = both[0:16, :] + (both[16:32, :] + cross)
    for a, b in ((1, 2), (0, 2), (1, 1), (1, 3), (1, 0), (0, 1), (0, 3)):
        i = a * 4 + b - 1
        cp = remote(
            dpart, rd.at[i], rd_s.at[i], rd_r.at[i], dev((zl + a) % 2, (x + b) % 4, y, z, p)
        )
        cp.start()
        sends.append(cp)
    for t in range(8):
        w = 2 * t
        k1 = (w % 4) * 4 + w // 4
        k2 = k1 + 4
        one = gfull[:, 128 * (k1 // 2):128 * (k1 // 2) + 128]
        two = gfull[:, 128 * (k2 // 2):128 * (k2 // 2) + 128]
        if k1 % 2:
            one = pltpu.roll(one, 64, 1)
        else:
            two = pltpu.roll(two, 64, 1)
        grad_ref[:, 128 * t:128 * t + 128] = jnp.where(left, one, two)
    for i in range(7):
        arrived(rd.at[i], rd_s.at[i], rd_r.at[i])
    total = jnp.zeros((16, 512), F32)
    for q in range(8):
        a, b = (zl + 2 - q // 4) % 2, (x + 4 - q % 4) % 4
        slot = a * 4 + b
        keep = jnp.where(slot == 0, dpart[...], rd[jnp.maximum(slot - 1, 0)])
        total = total + keep
    diag_row = c * 16 + lax.broadcasted_iota(jnp.int32, (16, 512), 0)
    diag_col = lax.broadcasted_iota(jnp.int32, (16, 512), 1)
    diag_ref[...] = jnp.where(diag_row >= diag_col, -total, 0.0)

    drain()


def body(adj_trailing, panel, panel_adjoint, inverse_diag):
    vmem, dma = pltpu.VMEM, pltpu.SemaphoreType.DMA
    operands = (adj_trailing, panel.T, panel_adjoint.T, inverse_diag)
    grad, diag = pl.pallas_call(
        kernel,
        out_shape=(
            jax.ShapeDtypeStruct((16, 1024), F32),
            jax.ShapeDtypeStruct((16, 512), F32),
        ),
        in_specs=[pl.BlockSpec(memory_space=pl.ANY)] * 4,
        out_specs=(pl.BlockSpec(memory_space=vmem), pl.BlockSpec(memory_space=vmem)),
        scratch_shapes=[
            vmem((16, 1024), F32), vmem((16, 1024), F32), vmem((512, 512), F32), vmem((128, 1024), F32),
            vmem((2, 1024, 256), F32), vmem((16, 2, 16, 1024), F32), vmem((256, 512), F32),
            vmem((1024, 512), BF16), vmem((1024, 512), BF16), vmem((512, 1024), BF16), vmem((512, 1024), BF16),
            vmem((256, 1024), BF16), vmem((256, 1024), BF16), vmem((512, 1024), BF16), vmem((512, 1024), BF16),
            vmem((512, 512), F32), vmem((256, 512), BF16), vmem((256, 512), BF16),
            vmem((256, 512), BF16), vmem((256, 512), BF16), vmem((1024, 128), F32),
            vmem((1024, 256), F32), vmem((512, 256), F32), vmem((4, 2, 128, 256), F32), vmem((7, 64, 256), F32),
            vmem((64, 512), F32), vmem((128, 128), F32), vmem((16, 8, 128), F32),
            vmem((2, 128, 512), F32), vmem((2, 256, 128), F32), vmem((2, 16, 16, 128), F32), vmem((16, 1024), F32),
            vmem((16, 512), F32), vmem((7, 16, 512), F32),
            dma((4,)), dma((4,)), dma((4,)), dma((4, 4)), dma((4, 4)), dma, dma, dma((4,)), dma((2, 2)),
            dma((2, 4)), dma((2, 4)), dma, dma,
            dma((4, 2)), dma((4, 2)), dma((7,)), dma((7,)), dma((3,)), dma((3,)), dma((16,)), dma((16,)),
            dma((2, 16)), dma((2, 16)), dma((7,)), dma((7,)),
        ],
        compiler_params=pltpu.CompilerParams(
            collective_id=0, has_side_effects=True, vmem_limit_bytes=40 * 1024 * 1024
        ),
        name="cholesky_step",
    )(*(pltpu.with_memory_space_constraint(a, pltpu.HBM) for a in operands))
    return (grad.T, diag)


def solution(mesh):
    in_specs = (P("row", "col"), P("row", "col"), P("row", "col"), P())
    out_specs = (P("row", "col"), P("col", None))
    return jax.shard_map(body, mesh=mesh, in_specs=in_specs, out_specs=out_specs, check_vma=False)
```
